1024 devices in a mesh: seq: 16 (over y, core), head: 4 (over x), dp: 16 (over z).
Axes of the slice: x: 4, y: 8, z: 16, core: 2. Of those that a mesh axis runs over, the one named last changes fastest.
Arguments:
- queries: bfloat16 [16, 3584, 4096], P('dp', 'seq', 'head'), may hold values from -6 to 6
- keys_in: bfloat16 [16, 3584, 4096], P('dp', 'seq', 'head'), may hold values from -6 to 6
- values_in: bfloat16 [16, 3584, 4096], P('dp', 'seq', 'head'), may hold values from -6 to 6
- grad_output: bfloat16 [16, 3584, 4096], P('dp', 'seq', 'head'), may hold values from -6 to 6
- log_decay: float32 [16, 3584, 32], P('dp', 'seq', 'head'), may hold values from -1 to 0, as said below
- doc_lengths: int32 [16, 4], P('dp'), may hold values from 1 to 1792, 3584 in all within a row
- norm_gain: float32 [4096], P('head'), may hold values from 0.1 to 1.9
Outputs:
- query_grad: bfloat16 [16, 3584, 4096], P('dp', 'seq', 'head')
- key_grad: bfloat16 [16, 3584, 4096], P('dp', 'seq', 'head')
- value_grad: bfloat16 [16, 3584, 4096], P('dp', 'seq', 'head')
- gain_grad: float32 [4096], P('head')
The draws below stay inside these ranges and needn't reach their ends.
Inputs may be any that keep to these rules, and one draw needn't show every extreme that they name: `doc_lengths`: each row holds 4 lengths that sum to 3584; the largest is exactly 1792. `log_decay`: every entry is negative.
All inputs are finite; a program needn't handle non-finite values.
Results may differ from the reference program's by a relative error of at most 0.0062.
Values sent between devices are 32-bit elements; how exact they have to be, the bound alone decides.
A program may use at most 64 MiB of HBM per device.

```python
import math
import jax
import jax.numpy as jnp
import numpy as np
from jax import lax

HD = 128
HEADS = 32
BLK = 224
DOCS = 4
SEQUENCE_LENGTH = 3584
BATCH_SEQUENCES = 16
WIDTH = 4096


def draw_log_decay(key, part):
    key = jax.random.fold_in(key, 7)
    selection_random_key, quick_random_key, gradual_random_key, noisy_random_key, spike_random_key, objective_random_key = jax.random.split(key, 6)
    fast_share = 0.5
    fast = jax.random.uniform(selection_random_key, (BATCH_SEQUENCES, 1, HEADS)) < fast_share
    fast_rate = jnp.exp(jax.random.uniform(quick_random_key, (BATCH_SEQUENCES, 1, HEADS), minval=math.log(1.0 / 50.0), maxval=math.log(1.0 / 30.0)))
    slow_rate = jnp.exp(jax.random.uniform(gradual_random_key, (BATCH_SEQUENCES, 1, HEADS), minval=math.log(0.15), maxval=math.log(0.7))) / SEQUENCE_LENGTH
    decay_speed = jnp.where(fast, fast_rate, slow_rate)
    noisy_values = jnp.exp(jax.random.uniform(noisy_random_key, (BATCH_SEQUENCES, SEQUENCE_LENGTH, HEADS), minval=-0.7, maxval=0.7))
    spike_values = jax.random.uniform(spike_random_key, (BATCH_SEQUENCES, SEQUENCE_LENGTH, 1)) < 2.0 / SEQUENCE_LENGTH
    objective_value = jnp.log(jax.random.uniform(objective_random_key, (BATCH_SEQUENCES, SEQUENCE_LENGTH, HEADS), minval=0.5, maxval=0.8))
    return (-decay_speed * noisy_values + jnp.where(spike_values, objective_value, 0.0)).astype(jnp.float32)


def levels(stream_key, shape, cuts, smallest, high):
    loudness = 1.0
    for axis_at, blocks in cuts:
        draws = jax.random.uniform(jax.random.fold_in(jax.random.fold_in(stream_key, 6), axis_at), (blocks,), jnp.float32, smallest / len(cuts), high / len(cuts))
        loudness = loudness * jnp.repeat(jnp.exp(draws), shape[axis_at] // blocks).reshape((-1,) + (1,) * (len(shape) - 1 - axis_at))
    return loudness


def length_profile(number_of, total, bound, skew):
    portions = [(1 << 20) // math.isqrt(standing ** skew) + 1 for standing in range(2, number_of + 1)]
    surplus, counts = total - bound - (number_of - 1), [1] * (number_of - 1)
    while surplus > 0:
        candidates = [i for i in range(number_of - 1) if counts[i] < bound]
        pool, budget = sum([portions[i] for i in candidates]), surplus
        for i in candidates:
            more = min(bound - counts[i], max(1, budget * portions[i] // pool), surplus)
            counts[i] = counts[i] + more
            surplus = surplus - more
    return np.array([bound] + counts)


def uneven(rng, amount, total, reach, skew):
    if amount == 2:
        one = jax.random.randint(rng, (), max(1, total - reach), min(reach, total - 1) + 1)
        return jnp.stack([one, total - one])
    tallies = jnp.asarray(length_profile(amount, total, reach, skew), jnp.int32)
    couples = (amount - 1) // 2
    donor, sink = tallies[1:1 + 2 * couples:2], tallies[2:2 + 2 * couples:2]
    margin = jnp.minimum(donor - 1, reach - sink)
    shifted = jax.random.randint(jax.random.fold_in(rng, 1), (couples,), 0, 1 << 20) % (margin + 1)
    tallies = tallies.at[1:1 + 2 * couples:2].set(donor - shifted).at[2:2 + 2 * couples:2].set(sink + shifted)
    return tallies[jax.random.permutation(jax.random.fold_in(rng, 2), amount)]


def normal_values(own_key, shape, scale, reach, cuts=(), held_as=jnp.bfloat16):
    drawn = scale * jax.random.normal(own_key, shape, jnp.float32)
    if cuts:
        drawn = drawn * levels(own_key, shape, cuts, -0.22, 0.18)
    return jnp.clip(drawn, -reach, reach).astype(held_as)


def setup_inputs(seed: int = 0) -> dict:
    key_list = jax.random.split(jax.random.key(seed), 8)
    return {
        "queries": normal_values(key_list[0], (BATCH_SEQUENCES, SEQUENCE_LENGTH, WIDTH), 1.0, 6.0, ((0, 16), (1, 16), (2, 4))),
        "keys_in": normal_values(key_list[1], (BATCH_SEQUENCES, SEQUENCE_LENGTH, WIDTH), 1.0, 6.0, ((0, 16), (1, 16), (2, 4))),
        "values_in": normal_values(key_list[2], (BATCH_SEQUENCES, SEQUENCE_LENGTH, WIDTH), 1.0, 6.0, ((0, 16), (1, 16), (2, 4))),
        "grad_output": normal_values(key_list[3], (BATCH_SEQUENCES, SEQUENCE_LENGTH, WIDTH), 1.0, 6.0, ((0, 16), (1, 16), (2, 4))),
        "log_decay": draw_log_decay(jax.random.fold_in(key_list[7], 71), 0),
        "doc_lengths": jax.vmap(lambda own: uneven(own, DOCS, SEQUENCE_LENGTH, SEQUENCE_LENGTH // 2, 2))(jax.random.split(key_list[5], BATCH_SEQUENCES)).reshape((BATCH_SEQUENCES, DOCS)).astype(jnp.int32),
        "norm_gain": jnp.clip(1.0 + 0.18 * jax.random.normal(key_list[6], (WIDTH,), jnp.float32), 0.1, 1.9),
    }


EPSILON = 1e-06

def widen(array):
    return array.astype(jnp.float32)

def block_terms(log_decay, resets):
    nblk, blk, heads = log_decay.shape
    zcount = jnp.cumsum(resets.astype(jnp.int32), axis=1, dtype=jnp.int32)
    cumlog = jnp.cumsum(log_decay, axis=1)
    keeping = (zcount == 0).astype(jnp.float32)
    entry = jnp.exp(cumlog) * keeping[:, :, None]
    tail = cumlog[:, -1:, :]
    ending = (zcount == zcount[:, -1:]).astype(jnp.float32)
    leaving = jnp.exp(tail - cumlog) * ending[:, :, None]
    carry_factor = jnp.exp(tail[:, 0, :]) * keeping[:, -1:]
    row_index = lax.broadcasted_iota(jnp.int32, (blk, blk), 0)
    col_index = lax.broadcasted_iota(jnp.int32, (blk, blk), 1)
    allowed = (zcount[:, :, None] == zcount[:, None, :]) & (col_index <= row_index)[None]
    allowed = allowed[:, None]
    by_head = jnp.transpose(cumlog, (0, 2, 1))
    spread = by_head[:, :, :, None] - by_head[:, :, None, :]
    decay_mask = jnp.where(allowed, jnp.exp(jnp.where(allowed, spread, 0.0)), 0.0)
    return (entry, leaving, carry_factor, decay_mask)

def forward_blocks(query, keys, values, entry, leaving, decay_mask):
    scores = jnp.einsum('bthd,bshd->bhts', widen(query), widen(keys))
    weights = (scores * decay_mask).astype(jnp.bfloat16)
    query_entry = (query * entry[..., None]).astype(jnp.bfloat16)
    key_leave = (keys * leaving[..., None]).astype(jnp.bfloat16)
    block_state = jnp.einsum('bshi,bshj->bhij', widen(key_leave), widen(values))
    return (weights, query_entry, block_state)

def chain_states(carry_factor, updates, initial, backward):

    def advance(state, pair):
        factor, update = pair
        return (factor[:, None, None] * state + update, state)
    return lax.scan(advance, initial, (carry_factor, updates), reverse=backward)

def attend(weights, values, query_entry, state_low):
    near = jnp.einsum('bhts,bshd->bthd', widen(weights), widen(values))
    far = jnp.einsum('bthi,bhij->bthj', widen(query_entry), widen(state_low))
    return near + far

def gradients(query, keys, values, grad_blocks, weights, decay_mask, entry, leaving, state_low, grad_low):
    raw = jnp.einsum('bthj,bshj->bhts', widen(grad_blocks), widen(values))
    masked = (raw * decay_mask).astype(jnp.bfloat16)
    query_part = jnp.einsum('bhts,bshi->bthi', widen(masked), widen(keys))
    query_part = query_part + entry[..., None] * jnp.einsum('bthj,bhij->bthi', widen(grad_blocks), widen(state_low))
    key_part = jnp.einsum('bhts,bthi->bshi', widen(masked), widen(query))
    key_part = key_part + leaving[..., None] * jnp.einsum('bshj,bhij->bshi', widen(values), widen(grad_low))
    value_part = jnp.einsum('bhts,bthj->bshj', widen(weights), widen(grad_blocks))
    value_part = value_part + leaving[..., None] * jnp.einsum('bshi,bhij->bshj', widen(keys), widen(grad_low))
    return (query_part.astype(jnp.bfloat16), key_part.astype(jnp.bfloat16), value_part.astype(jnp.bfloat16))

def reference(queries, keys_in, values_in, grad_output, log_decay, doc_lengths, norm_gain):
    nblk = SEQUENCE_LENGTH // BLK
    shape4 = (nblk, BLK, HEADS, HD)

    def single_sequence(items):
        query_row, key_row, value_row, upstream_row, decay_row, lengths = items
        query = query_row.reshape(shape4)
        keys = key_row.reshape(shape4)
        values = value_row.reshape(shape4)
        decay = decay_row.reshape(nblk, BLK, HEADS)
        positions = jnp.arange(SEQUENCE_LENGTH, dtype=jnp.int32)
        starts = jnp.cumsum(lengths, dtype=jnp.int32) - lengths
        resets = jnp.any(positions[:, None] == starts[None, 1:], axis=1).reshape(nblk, BLK)
        entry, leaving, carry_factor, decay_mask = block_terms(decay, resets)
        weights, query_entry, block_state = forward_blocks(query, keys, values, entry, leaving, decay_mask)
        empty = jnp.zeros((HEADS, HD, HD), jnp.float32)
        _, before = chain_states(carry_factor, block_state, empty, False)
        state_low = before.astype(jnp.bfloat16)
        attn = attend(weights, values, query_entry, state_low).reshape(SEQUENCE_LENGTH, WIDTH)
        upstream = upstream_row.astype(jnp.float32)
        scaled = upstream * norm_gain[None, :]
        squares = lax.optimization_barrier(jnp.sum(attn * attn, axis=1))
        inner = lax.optimization_barrier(jnp.sum(scaled * attn, axis=1))
        recip = lax.rsqrt(squares / WIDTH + EPSILON)
        coef = recip * recip * recip * inner / WIDTH
        grad_attn = (recip[:, None] * scaled - coef[:, None] * attn).astype(jnp.bfloat16)
        gain_part = lax.optimization_barrier(jnp.sum(upstream * attn * recip[:, None], axis=0))
        grad_blocks = grad_attn.reshape(shape4)
        grad_update = jnp.einsum('bthi,bthj->bhij', widen(query_entry), widen(grad_blocks))
        _, after = chain_states(carry_factor, grad_update, empty, True)
        grad_low = after.astype(jnp.bfloat16)
        query_part, key_part, value_part = gradients(query, keys, values, grad_blocks, weights, decay_mask, entry, leaving, state_low, grad_low)
        return (query_part.reshape(SEQUENCE_LENGTH, WIDTH), key_part.reshape(SEQUENCE_LENGTH, WIDTH), value_part.reshape(SEQUENCE_LENGTH, WIDTH), gain_part)
    query_grad, key_grad, value_grad, gain_parts = lax.map(single_sequence, (queries, keys_in, values_in, grad_output, log_decay, doc_lengths))
    gain_grad = lax.optimization_barrier(jnp.sum(gain_parts, axis=0)) / math.sqrt(BATCH_SEQUENCES * SEQUENCE_LENGTH)
    return (query_grad, key_grad, value_grad, gain_grad)
```

```python
import functools
import math

import jax
import jax.numpy as jnp
from jax import lax
from jax.experimental import pallas as pl
from jax.experimental.pallas import tpu as pltpu
from jax.sharding import PartitionSpec as P

EPSILON = 1e-06
HD = 128
TAG = 8
SPLIT = 2
UNROLL = 2
MESH = pl.DeviceIdType.MESH
EXACT = lax.Precision.HIGHEST
F32 = jnp.float32
BF16 = jnp.bfloat16


def dot(left, right, over_left, over_right, precision=None):
    return lax.dot_general(
        left,
        right,
        (((over_left,), (over_right,)), ((), ())),
        preferred_element_type=F32,
        precision=precision,
    )


def each_head(body, start, count):
    def turn(step, carried):
        body([start + step * UNROLL + one for one in range(UNROLL)])
        return carried

    lax.fori_loop(0, count // UNROLL, turn, 0)


def kernel(
    seqs,
    teams,
    q_hbm,
    k_hbm,
    v_hbm,
    up_hbm,
    log_hbm,
    lengths,
    gain_in,
    q_out,
    k_out,
    v_out,
    gain_out,
    q_ref,
    k_ref,
    v_ref,
    up_ref,
    log_ref,
    c_row,
    c_col,
    bias_ref,
    enter_ref,
    leave_ref,
    decay_ref,
    weight_ref,
    entered_ref,
    attn_ref,
    grad_ref,
    squares_ref,
    inner_ref,
    k_part,
    v_part,
    own_ref,
    peer_ref,
    chain_in,
    chain_out,
    pass_ref,
    far_ref,
    state_ref,
    sums_ref,
    sums_in,
    load_sem,
    pair_send,
    pair_recv,
    chain_send,
    chain_recv,
    pass_send,
    pass_recv,
    sums_send,
    sums_recv,
):
    blk, features = q_ref.shape
    heads = features // HD
    half = heads // 2
    chunks = half * SPLIT
    span = HD // SPLIT
    chips = seqs // 2
    seq = lax.axis_index("seq")
    team = lax.axis_index("head")
    core = lax.rem(seq, 2)
    chip = lax.div(seq, 2)
    other = 1 - core
    peer = seq + 1 - 2 * core

    loads = [
        pltpu.make_async_copy(source.at[0], target, load_sem.at[slot])
        for slot, (source, target) in enumerate(
            [(log_hbm, log_ref), (k_hbm, k_ref), (v_hbm, v_ref), (q_hbm, q_ref), (up_hbm, up_ref)]
        )
    ]
    for load in loads:
        load.start()

    barrier = pltpu.get_barrier_semaphore()
    pl.semaphore_signal(barrier, inc=1, device_id={"seq": peer}, device_id_type=MESH)
    for step in range(1, teams):
        pl.semaphore_signal(
            barrier, inc=1, device_id={"head": lax.rem(team + step, teams)}, device_id_type=MESH
        )

    @pl.when(chip > 0)
    def _():
        pl.semaphore_signal(barrier, inc=1, device_id={"seq": seq - 2}, device_id_type=MESH)

    @pl.when(chip < chips - 1)
    def _():
        pl.semaphore_signal(barrier, inc=1, device_id={"seq": seq + 2}, device_id_type=MESH)

    def lanes(head):
        return pl.ds(pl.multiple_of(head * HD, HD), HD)

    row = lax.broadcasted_iota(jnp.int32, (blk, blk), 0)
    col = lax.broadcasted_iota(jnp.int32, (blk, blk), 1)
    triangle = (col <= row).astype(F32)
    places = []
    total = 0
    for one in range(lengths.shape[1] - 1):
        total = total + lengths[0, one]
        place = total - seq * blk
        places.append(jnp.where(place < 0, 2 * blk, place))
    at_row = lax.broadcasted_iota(jnp.int32, (blk, 1), 0)
    at_col = lax.broadcasted_iota(jnp.int32, (1, blk), 1)
    z_row = sum((at_row >= place).astype(jnp.int32) for place in places)
    z_col = sum((at_col >= place).astype(jnp.int32) for place in places)
    z_end = sum(jnp.where(place < blk, 1, 0) for place in places)
    loads[0].wait()
    log = log_ref[...]
    c_all = dot(triangle, log, 1, 1, EXACT)
    tail = c_all[blk - 1 : blk, :]
    leaving = jnp.exp(tail - c_all) * (z_row == z_end).astype(F32)
    carry = jnp.exp(tail) * jnp.where(z_end == 0, 1.0, 0.0)
    for head in range(heads):
        leave_ref[head] = jnp.broadcast_to(leaving[:, head : head + 1], (blk, HD))
        tag = jnp.broadcast_to(carry[:, head : head + 1], (TAG, HD))
        own_ref[0, head, HD : HD + TAG, :] = tag
        own_ref[1, head, HD : HD + TAG, :] = tag

    def block_state(group):
        made = []
        for head in group:
            left = (k_ref[:, lanes(head)].astype(F32) * leave_ref[head]).astype(BF16)
            made.append(dot(left, v_ref[:, lanes(head)], 0, 0))
        for head, value in zip(group, made):
            own_ref[0, head, 0:HD, :] = value

    def exchange(way):
        return pltpu.make_async_remote_copy(
            src_ref=own_ref.at[way, pl.ds(other * half, half)],
            dst_ref=peer_ref.at[way],
            send_sem=pair_send.at[way],
            recv_sem=pair_recv.at[way],
            device_id={"seq": peer},
            device_id_type=MESH,
        )

    def ahead(way, index, to):
        at = (way, lax.div(index, SPLIT), pl.ds(pl.multiple_of(lax.rem(index, SPLIT) * span, span), span))
        return pltpu.make_async_remote_copy(
            src_ref=chain_out.at[at],
            dst_ref=chain_in.at[at],
            send_sem=chain_send.at[way, index],
            recv_sem=chain_recv.at[way, index],
            device_id={"seq": to},
            device_id_type=MESH,
        )

    def across(way, index):
        at = (way, lax.div(index, SPLIT), pl.ds(pl.multiple_of(lax.rem(index, SPLIT) * span, span), span))
        return pltpu.make_async_remote_copy(
            src_ref=pass_ref.at[at],
            dst_ref=far_ref.at[at],
            send_sem=pass_send.at[way, index],
            recv_sem=pass_recv.at[way, index],
            device_id={"seq": peer},
            device_id_type=MESH,
        )

    def chain(way, first, has_prev, has_next, to):
        exchange(way).wait_recv()

        def joined(local, carried):
            mine = own_ref[way, core * half + local, 0:HD, :]
            theirs = peer_ref[way, local, 0:HD, :]
            my_carry = own_ref[way, core * half + local, HD : HD + 1, :]
            their_carry = peer_ref[way, local, HD : HD + 1, :]
            chain_out[way, local] = jnp.where(
                first, their_carry * mine + theirs, my_carry * theirs + mine
            )
            return carried

        @pl.when(has_next)
        def _():
            lax.fori_loop(0, half, joined, 0)

        @pl.when(jnp.logical_not(has_prev))
        def _():
            chain_in[way] = jnp.zeros(chain_in.shape[1:], F32)

        def turn(index, carried):
            local = lax.div(index, SPLIT)
            rows = pl.ds(pl.multiple_of(lax.rem(index, SPLIT) * span, span), span)
            my_carry = own_ref[way, core * half + local, HD : HD + 1, :]
            their_carry = peer_ref[way, local, HD : HD + 1, :]

            @pl.when(has_prev)
            def _():
                ahead(way, index, to).wait_recv()

            state = chain_in[way, local, rows, :]

            @pl.when(has_next)
            def _():
                chain_out[way, local, rows, :] = (
                    my_carry * their_carry * state + chain_out[way, local, rows, :]
                )
                ahead(way, index, to).start()

            mine = own_ref[way, core * half + local, rows, :]
            theirs = peer_ref[way, local, rows, :]
            middle = jnp.where(first, my_carry * state + mine, their_carry * state + theirs)
            pass_ref[way, local, rows, :] = jnp.where(first, middle, state)
            across(way, index).start()
            state_ref[way, core * half + local, rows, :] = jnp.where(first, state, middle).astype(BF16)
            return carried

        lax.fori_loop(0, chunks, turn, 0)

        def land(index, carried):
            local = lax.div(index, SPLIT)
            rows = pl.ds(pl.multiple_of(lax.rem(index, SPLIT) * span, span), span)
            across(way, index).wait_recv()
            state_ref[way, other * half + local, rows, :] = far_ref[way, local, rows, :].astype(BF16)
            return carried

        lax.fori_loop(0, chunks, land, 0)

    loads[1].wait()
    loads[2].wait()
    each_head(block_state, other * half, half)
    pl.semaphore_wait(
        barrier, teams + jnp.where(chip > 0, 1, 0) + jnp.where(chip < chips - 1, 1, 0)
    )
    exchange(0).start()
    each_head(block_state, core * half, half)

    c_row[...] = dot(log, triangle, 1, 1, EXACT)
    entering = jnp.exp(c_all) * (z_row == 0).astype(F32)
    for head in range(heads):
        enter_ref[head] = jnp.broadcast_to(entering[:, head : head + 1], (blk, HD))
        c_col[head] = jnp.broadcast_to(c_all[:, head : head + 1], (blk, HD))
    bias_ref[...] = jnp.where((z_row == z_col) & (col <= row), 0.0, -1e30)
    loads[3].wait()
    loads[4].wait()

    def near(group):
        made = []
        for head in group:
            query = q_ref[:, lanes(head)]
            scores = dot(query, k_ref[:, lanes(head)], 1, 1)
            start = jnp.broadcast_to(c_col[head][:, 0:1], (blk, blk))
            decay = jnp.exp(start - c_row[pl.ds(head, 1), :] + bias_ref[...])
            weight = (scores * decay).astype(BF16)
            entered = (query.astype(F32) * enter_ref[head]).astype(BF16)
            made.append((decay, weight, entered, dot(weight, v_ref[:, lanes(head)], 1, 0)))
        for head, (decay, weight, entered, value) in zip(group, made):
            decay_ref[head] = decay
            weight_ref[head] = weight
            entered_ref[head] = entered
            attn_ref[head] = value

    early = chips // 2 - 1

    @pl.when(chip >= early)
    def _():
        each_head(near, 0, heads)

    chain(0, core == 0, chip > 0, chip < chips - 1, lax.rem(seq + 2, seqs))

    @pl.when(chip < early)
    def _():
        each_head(near, 0, heads)

    squares_ref[...] = jnp.zeros_like(squares_ref)
    inner_ref[...] = jnp.zeros_like(inner_ref)

    def attend(group):
        squares, inner = squares_ref[...], inner_ref[...]
        made = []
        for head in group:
            attn = attn_ref[head] + dot(entered_ref[head], state_ref[0, head], 1, 0)
            scaled = up_ref[:, lanes(head)].astype(F32) * gain_in[pl.ds(head, 1), :]
            squares = squares + attn * attn
            inner = inner + scaled * attn
            made.append(attn)
        for head, attn in zip(group, made):
            attn_ref[head] = attn
        squares_ref[...] = squares
        inner_ref[...] = inner

    each_head(attend, 0, heads)
    ones = jnp.ones((8, HD), F32)
    sums_ref[0:8, :] = dot(ones, squares_ref[...], 1, 1, EXACT)
    sums_ref[8:16, :] = dot(ones, inner_ref[...], 1, 1, EXACT)
    shares = [
        pltpu.make_async_remote_copy(
            src_ref=sums_ref,
            dst_ref=sums_in.at[step - 1],
            send_sem=sums_send.at[step - 1],
            recv_sem=sums_recv.at[step - 1],
            device_id={"head": lax.rem(team + step, teams)},
            device_id_type=MESH,
        )
        for step in range(1, teams)
    ]
    for share in shares:
        share.start()
    for share in shares:
        share.wait_recv()
    sums = sums_ref[...]
    for step in range(1, teams):
        sums = sums + sums_in[step - 1]
    width = features * teams
    chosen = lax.broadcasted_iota(jnp.int32, (8, HD), 0)
    chosen = jnp.where(chosen == 0, 1.0, 0.0).astype(F32)
    squares = dot(sums[0:8, :], chosen, 0, 0, EXACT)
    inner = dot(sums[8:16, :], chosen, 0, 0, EXACT)
    recip = lax.rsqrt(squares / width + EPSILON)
    squares_ref[...] = recip
    inner_ref[...] = recip * recip * recip * inner / width

    def gradient(group):
        recip, coef = squares_ref[...], inner_ref[...]
        made = []
        for head in group:
            attn = attn_ref[head]
            upstream = up_ref[:, lanes(head)].astype(F32)
            scaled = upstream * gain_in[pl.ds(head, 1), :]
            grad = (recip * scaled - coef * attn).astype(BF16)
            part = jnp.sum(upstream * attn * recip, axis=0, keepdims=True)
            made.append((grad, part, dot(entered_ref[head], grad, 0, 0)))
        for head, (grad, part, value) in zip(group, made):
            grad_ref[head] = grad
            gain_out[pl.ds(head, 1), :] = part
            own_ref[1, head, 0:HD, :] = value

    each_head(gradient, other * half, half)
    exchange(1).start()
    each_head(gradient, core * half, half)

    def masked(group):
        made = []
        for head in group:
            grad = grad_ref[head]
            raw = dot(grad, v_ref[:, lanes(head)], 1, 1)
            mask = (raw * decay_ref[head]).astype(BF16)
            query = dot(mask, k_ref[:, lanes(head)], 1, 0)
            query = query + enter_ref[head] * dot(grad, state_ref[0, head], 1, 1)
            made.append(
                (
                    query.astype(BF16),
                    dot(mask, q_ref[:, lanes(head)], 0, 0),
                    dot(weight_ref[head], grad, 0, 0),
                )
            )
        for head, (query, key, value) in zip(group, made):
            q_out[0, :, lanes(head)] = query
            k_part[head] = key
            v_part[head] = value

    late = chips - early

    @pl.when(chip < late)
    def _():
        each_head(masked, 0, heads)

    chain(1, core == 1, chip < chips - 1, chip > 0, lax.rem(seq + seqs - 2, seqs))

    @pl.when(chip >= late)
    def _():
        each_head(masked, 0, heads)

    def finish(group):
        made = []
        for head in group:
            state = state_ref[1, head]
            leave = leave_ref[head]
            key = k_part[head] + leave * dot(v_ref[:, lanes(head)], state, 1, 1)
            value = v_part[head] + leave * dot(k_ref[:, lanes(head)], state, 1, 0)
            made.append((key.astype(BF16), value.astype(BF16)))
        for head, (key, value) in zip(group, made):
            k_out[0, :, lanes(head)] = key
            v_out[0, :, lanes(head)] = value

    each_head(finish, 0, heads)

    for share in shares:
        share.wait_send()
    for way, has_next in ((0, chip < chips - 1), (1, chip > 0)):
        exchange(way).wait_send()

        def sent(index, carried, way=way, has_next=has_next):
            @pl.when(has_next)
            def _():
                ahead(way, index, peer).wait_send()

            across(way, index).wait_send()
            return carried

        lax.fori_loop(0, chunks, sent, 0)


def on_device(seqs, teams, queries, keys_in, values_in, grad_output, log_decay, lengths, norm_gain):
    tokens, features = queries.shape[1:]
    heads = log_decay.shape[2]
    half = heads // 2
    chunks = half * SPLIT
    whole = jax.ShapeDtypeStruct((1, tokens, features), BF16)
    anywhere = pl.BlockSpec(memory_space=pltpu.HBM)
    vmem = pl.BlockSpec(memory_space=pltpu.VMEM)
    wide = pltpu.VMEM((heads, tokens, HD), F32)
    states = pltpu.VMEM((2, half, HD, HD), F32)
    query_grad, key_grad, value_grad, gain = pl.pallas_call(
        functools.partial(kernel, seqs, teams),
        out_shape=(whole, whole, whole, jax.ShapeDtypeStruct((heads, HD), F32)),
        in_specs=[anywhere] * 5 + [pl.BlockSpec(memory_space=pltpu.SMEM), vmem],
        out_specs=[vmem] * 4,
        scratch_shapes=[
            pltpu.VMEM((tokens, features), BF16),
            pltpu.VMEM((tokens, features), BF16),
            pltpu.VMEM((tokens, features), BF16),
            pltpu.VMEM((tokens, features), BF16),
            pltpu.VMEM((heads, tokens), F32),
            pltpu.VMEM((heads, tokens), F32),
            wide,
            pltpu.VMEM((tokens, tokens), F32),
            wide,
            wide,
            pltpu.VMEM((heads, tokens, tokens), F32),
            pltpu.VMEM((heads, tokens, tokens), BF16),
            pltpu.VMEM((heads, tokens, HD), BF16),
            wide,
            pltpu.VMEM((heads, tokens, HD), BF16),
            pltpu.VMEM((tokens, HD), F32),
            pltpu.VMEM((tokens, HD), F32),
            wide,
            wide,
            pltpu.VMEM((2, heads, HD + TAG, HD), F32),
            pltpu.VMEM((2, half, HD + TAG, HD), F32),
            states,
            states,
            states,
            states,
            pltpu.VMEM((2, heads, HD, HD), BF16),
            pltpu.VMEM((16, tokens), F32),
            pltpu.VMEM((teams - 1, 16, tokens), F32),
            pltpu.SemaphoreType.DMA((5,)),
            pltpu.SemaphoreType.DMA((2,)),
            pltpu.SemaphoreType.DMA((2,)),
            pltpu.SemaphoreType.DMA((2, chunks)),
            pltpu.SemaphoreType.DMA((2, chunks)),
            pltpu.SemaphoreType.DMA((2, chunks)),
            pltpu.SemaphoreType.DMA((2, chunks)),
            pltpu.SemaphoreType.DMA((teams - 1,)),
            pltpu.SemaphoreType.DMA((teams - 1,)),
        ],
        compiler_params=pltpu.CompilerParams(
            collective_id=0, has_side_effects=True, vmem_limit_bytes=48 * 1024 * 1024
        ),
    )(
        queries,
        keys_in,
        values_in,
        grad_output,
        jnp.swapaxes(log_decay, 1, 2),
        lengths,
        norm_gain.reshape(heads, HD),
    )
    rows = tokens * seqs * lax.axis_size("dp")
    gain_grad = lax.psum(gain.reshape(features), ("seq", "dp")) / math.sqrt(rows)
    return query_grad, key_grad, value_grad, gain_grad


def solution(mesh):
    split = P("dp", "seq", "head")
    return jax.shard_map(
        functools.partial(on_device, mesh.shape["seq"], mesh.shape["head"]),
        mesh=mesh,
        in_specs=(split, split, split, split, split, P("dp", None), P("head")),
        out_specs=(split, split, split, P("head")),
        check_vma=False,
    )
```

```python
import functools
import math

import jax
import jax.numpy as jnp
from jax import lax
from jax.experimental import pallas as pl
from jax.experimental.pallas import tpu as pltpu
from jax.sharding import PartitionSpec as P

EPSILON = 1e-06
HD = 128
TAG = 8
SPLIT = 2
UNROLL = 2
MESH = pl.DeviceIdType.MESH
EXACT = lax.Precision.HIGHEST
F32 = jnp.float32
BF16 = jnp.bfloat16


def dot(left, right, over_left, over_right, precision=None):
    return lax.dot_general(
        left,
        right,
        (((over_left,), (over_right,)), ((), ())),
        preferred_element_type=F32,
        precision=precision,
    )


def each_head(body, start, count):
    def turn(step, carried):
        body([start + step * UNROLL + one for one in range(UNROLL)])
        return carried

    lax.fori_loop(0, count // UNROLL, turn, 0)


def kernel(
    seqs,
    teams,
    rows_of,
    q_hbm,
    k_hbm,
    v_hbm,
    up_hbm,
    log_hbm,
    lengths,
    gain_in,
    q_out,
    k_out,
    v_out,
    gain_out,
    q_ref,
    k_ref,
    v_ref,
    up_ref,
    log_ref,
    c_row,
    c_col,
    bias_ref,
    enter_ref,
    leave_ref,
    decay_ref,
    weight_ref,
    entered_ref,
    attn_ref,
    grad_ref,
    squares_ref,
    inner_ref,
    k_part,
    v_part,
    own_ref,
    peer_ref,
    chain_in,
    chain_out,
    pass_ref,
    far_ref,
    state_ref,
    sums_ref,
    sums_in,
    gain_row,
    gain_chips,
    gain_rows,
    gain_far,
    load_sem,
    pair_send,
    pair_recv,
    chain_send,
    chain_recv,
    pass_send,
    pass_recv,
    sums_send,
    sums_recv,
    gain_chips_send,
    gain_chips_recv,
    gain_rows_send,
    gain_rows_recv,
    gain_far_sem,
):
    blk, features = q_ref.shape
    heads = features // HD
    half = heads // 2
    chunks = half * SPLIT
    span = HD // SPLIT
    chips = seqs // 2
    seq = lax.axis_index("seq")
    team = lax.axis_index("head")
    place_z = lax.axis_index("dp")
    core = lax.rem(seq, 2)
    chip = lax.div(seq, 2)
    other = 1 - core
    peer = seq + 1 - 2 * core

    loads = [
        pltpu.make_async_copy(source.at[0], target, load_sem.at[slot])
        for slot, (source, target) in enumerate(
            [(log_hbm, log_ref), (k_hbm, k_ref), (v_hbm, v_ref), (q_hbm, q_ref), (up_hbm, up_ref)]
        )
    ]
    for load in loads:
        load.start()

    barrier = pltpu.get_barrier_semaphore()
    pl.semaphore_signal(barrier, inc=1, device_id={"seq": peer}, device_id_type=MESH)
    for step in range(1, teams):
        pl.semaphore_signal(
            barrier, inc=1, device_id={"head": lax.rem(team + step, teams)}, device_id_type=MESH
        )

    for step in range(1, chips):
        pl.semaphore_signal(
            barrier, inc=1, device_id={"seq": lax.rem(seq + 2 * step, seqs)}, device_id_type=MESH
        )

    def greet(step, carried):
        pl.semaphore_signal(
            barrier, inc=1, device_id={"dp": lax.rem(place_z + step, rows_of)}, device_id_type=MESH
        )
        return carried

    lax.fori_loop(1, rows_of, greet, 0)

    def lanes(head):
        return pl.ds(pl.multiple_of(head * HD, HD), HD)

    row = lax.broadcasted_iota(jnp.int32, (blk, blk), 0)
    col = lax.broadcasted_iota(jnp.int32, (blk, blk), 1)
    triangle = (col <= row).astype(F32)
    places = []
    total = 0
    for one in range(lengths.shape[1] - 1):
        total = total + lengths[0, one]
        place = total - seq * blk
        places.append(jnp.where(place < 0, 2 * blk, place))
    at_row = lax.broadcasted_iota(jnp.int32, (blk, 1), 0)
    at_col = lax.broadcasted_iota(jnp.int32, (1, blk), 1)
    z_row = sum((at_row >= place).astype(jnp.int32) for place in places)
    z_col = sum((at_col >= place).astype(jnp.int32) for place in places)
    z_end = sum(jnp.where(place < blk, 1, 0) for place in places)
    loads[0].wait()
    log = log_ref[...]
    c_all = dot(triangle, log, 1, 1, EXACT)
    tail = c_all[blk - 1 : blk, :]
    leaving = jnp.exp(tail - c_all) * (z_row == z_end).astype(F32)
    carry = jnp.exp(tail) * jnp.where(z_end == 0, 1.0, 0.0)
    for head in range(heads):
        leave_ref[head] = jnp.broadcast_to(leaving[:, head : head + 1], (blk, HD))
        tag = jnp.broadcast_to(carry[:, head : head + 1], (TAG, HD))
        own_ref[0, head, HD : HD + TAG, :] = tag
        own_ref[1, head, HD : HD + TAG, :] = tag

    def block_state(group):
        made = []
        for head in group:
            left = (k_ref[:, lanes(head)].astype(F32) * leave_ref[head]).astype(BF16)
            made.append(dot(left, v_ref[:, lanes(head)], 0, 0))
        for head, value in zip(group, made):
            own_ref[0, head, 0:HD, :] = value

    def exchange(way):
        return pltpu.make_async_remote_copy(
            src_ref=own_ref.at[way, pl.ds(other * half, half)],
            dst_ref=peer_ref.at[way],
            send_sem=pair_send.at[way],
            recv_sem=pair_recv.at[way],
            device_id={"seq": peer},
            device_id_type=MESH,
        )

    def ahead(way, index, to):
        at = (way, lax.div(index, SPLIT), pl.ds(pl.multiple_of(lax.rem(index, SPLIT) * span, span), span))
        return pltpu.make_async_remote_copy(
            src_ref=chain_out.at[at],
            dst_ref=chain_in.at[at],
            send_sem=chain_send.at[way, index],
            recv_sem=chain_recv.at[way, index],
            device_id={"seq": to},
            device_id_type=MESH,
        )

    def across(way, index):
        at = (way, lax.div(index, SPLIT), pl.ds(pl.multiple_of(lax.rem(index, SPLIT) * span, span), span))
        return pltpu.make_async_remote_copy(
            src_ref=pass_ref.at[at],
            dst_ref=far_ref.at[at],
            send_sem=pass_send.at[way, index],
            recv_sem=pass_recv.at[way, index],
            device_id={"seq": peer},
            device_id_type=MESH,
        )

    def join(way, first, has_next):
        exchange(way).wait_recv()

        def joined(local, carried):
            mine = own_ref[way, core * half + local, 0:HD, :]
            theirs = peer_ref[way, local, 0:HD, :]
            my_carry = own_ref[way, core * half + local, HD : HD + 1, :]
            their_carry = peer_ref[way, local, HD : HD + 1, :]
            chain_out[way, local] = jnp.where(
                first, their_carry * mine + theirs, my_carry * theirs + mine
            )
            return carried

        @pl.when(has_next)
        def _():
            lax.fori_loop(0, half, joined, 0)

    def chain(way, first, has_prev, has_next, to):
        @pl.when(jnp.logical_not(has_prev))
        def _():
            chain_in[way] = jnp.zeros(chain_in.shape[1:], F32)

        def turn(index, carried):
            local = lax.div(index, SPLIT)
            rows = pl.ds(pl.multiple_of(lax.rem(index, SPLIT) * span, span), span)
            my_carry = own_ref[way, core * half + local, HD : HD + 1, :]
            their_carry = peer_ref[way, local, HD : HD + 1, :]

            @pl.when(has_prev)
            def _():
                ahead(way, index, to).wait_recv()

            state = chain_in[way, local, rows, :]

            @pl.when(has_next)
            def _():
                chain_out[way, local, rows, :] = (
                    my_carry * their_carry * state + chain_out[way, local, rows, :]
                )
                ahead(way, index, to).start()

            mine = own_ref[way, core * half + local, rows, :]
            theirs = peer_ref[way, local, rows, :]
            middle = jnp.where(first, my_carry * state + mine, their_carry * state + theirs)
            pass_ref[way, local, rows, :] = jnp.where(first, middle, state)
            across(way, index).start()
            state_ref[way, core * half + local, rows, :] = jnp.where(first, state, middle).astype(BF16)
            return carried

        lax.fori_loop(0, chunks, turn, 0)

        def land(index, carried):
            local = lax.div(index, SPLIT)
            rows = pl.ds(pl.multiple_of(lax.rem(index, SPLIT) * span, span), span)
            across(way, index).wait_recv()
            state_ref[way, other * half + local, rows, :] = far_ref[way, local, rows, :].astype(BF16)
            return carried

        lax.fori_loop(0, chunks, land, 0)

    loads[1].wait()
    loads[2].wait()
    each_head(block_state, other * half, half)
    pl.semaphore_wait(barrier, 1 + teams - 1 + chips - 1 + rows_of - 1)
    exchange(0).start()
    each_head(block_state, core * half, half)

    c_row[...] = dot(log, triangle, 1, 1, EXACT)
    entering = jnp.exp(c_all) * (z_row == 0).astype(F32)
    for head in range(heads):
        enter_ref[head] = jnp.broadcast_to(entering[:, head : head + 1], (blk, HD))
        c_col[head] = jnp.broadcast_to(c_all[:, head : head + 1], (blk, HD))
    bias_ref[...] = jnp.where((z_row == z_col) & (col <= row), 0.0, -1e30)
    loads[3].wait()
    loads[4].wait()

    def near(group):
        made = []
        for head in group:
            query = q_ref[:, lanes(head)]
            scores = dot(query, k_ref[:, lanes(head)], 1, 1)
            start = jnp.broadcast_to(c_col[head][:, 0:1], (blk, blk))
            decay = jnp.exp(start - c_row[pl.ds(head, 1), :] + bias_ref[...])
            weight = (scores * decay).astype(BF16)
            entered = (query.astype(F32) * enter_ref[head]).astype(BF16)
            made.append((decay, weight, entered, dot(weight, v_ref[:, lanes(head)], 1, 0)))
        for head, (decay, weight, entered, value) in zip(group, made):
            decay_ref[head] = decay
            weight_ref[head] = weight
            entered_ref[head] = entered
            attn_ref[head] = value

    early = chips // 2 - 1

    @pl.when(chip >= early)
    def _():
        each_head(near, 0, heads)

    join(0, core == 0, chip < chips - 1)
    chain(0, core == 0, chip > 0, chip < chips - 1, lax.rem(seq + 2, seqs))

    @pl.when(chip < early)
    def _():
        each_head(near, 0, heads)

    squares_ref[...] = jnp.zeros_like(squares_ref)
    inner_ref[...] = jnp.zeros_like(inner_ref)

    def attend(group):
        squares, inner = squares_ref[...], inner_ref[...]
        made = []
        for head in group:
            attn = attn_ref[head] + dot(entered_ref[head], state_ref[0, head], 1, 0)
            scaled = up_ref[:, lanes(head)].astype(F32) * gain_in[pl.ds(head, 1), :]
            squares = squares + attn * attn
            inner = inner + scaled * attn
            made.append(attn)
        for head, attn in zip(group, made):
            attn_ref[head] = attn
        squares_ref[...] = squares
        inner_ref[...] = inner

    each_head(attend, 0, heads)
    ones = jnp.ones((8, HD), F32)
    sums_ref[0:8, :] = dot(ones, squares_ref[...], 1, 1, EXACT)
    sums_ref[8:16, :] = dot(ones, inner_ref[...], 1, 1, EXACT)
    shares = [
        pltpu.make_async_remote_copy(
            src_ref=sums_ref,
            dst_ref=sums_in.at[step - 1],
            send_sem=sums_send.at[step - 1],
            recv_sem=sums_recv.at[step - 1],
            device_id={"head": lax.rem(team + step, teams)},
            device_id_type=MESH,
        )
        for step in range(1, teams)
    ]
    for share in shares:
        share.start()
    for share in shares:
        share.wait_recv()
    sums = sums_ref[...]
    for step in range(1, teams):
        sums = sums + sums_in[step - 1]
    width = features * teams
    chosen = lax.broadcasted_iota(jnp.int32, (8, HD), 0)
    chosen = jnp.where(chosen == 0, 1.0, 0.0).astype(F32)
    squares = dot(sums[0:8, :], chosen, 0, 0, EXACT)
    inner = dot(sums[8:16, :], chosen, 0, 0, EXACT)
    recip = lax.rsqrt(squares / width + EPSILON)
    squares_ref[...] = recip
    inner_ref[...] = recip * recip * recip * inner / width

    def gradient(group):
        recip, coef = squares_ref[...], inner_ref[...]
        made = []
        for head in group:
            attn = attn_ref[head]
            upstream = up_ref[:, lanes(head)].astype(F32)
            scaled = upstream * gain_in[pl.ds(head, 1), :]
            grad = (recip * scaled - coef * attn).astype(BF16)
            part = jnp.sum(upstream * attn * recip, axis=0, keepdims=True)
            made.append((grad, part, dot(entered_ref[head], grad, 0, 0)))
        for head, (grad, part, value) in zip(group, made):
            grad_ref[head] = grad
            gain_row[pl.ds(head, 1), :] = part
            own_ref[1, head, HD + 1 : HD + 2, :] = part
            own_ref[1, head, 0:HD, :] = value

    each_head(gradient, other * half, half)
    exchange(1).start()
    each_head(gradient, core * half, half)

    def masked(group):
        made = []
        for head in group:
            grad = grad_ref[head]
            raw = dot(grad, v_ref[:, lanes(head)], 1, 1)
            mask = (raw * decay_ref[head]).astype(BF16)
            query = dot(mask, k_ref[:, lanes(head)], 1, 0)
            query = query + enter_ref[head] * dot(grad, state_ref[0, head], 1, 1)
            made.append(
                (
                    query.astype(BF16),
                    dot(mask, q_ref[:, lanes(head)], 0, 0),
                    dot(weight_ref[head], grad, 0, 0),
                )
            )
        for head, (query, key, value) in zip(group, made):
            q_out[0, :, lanes(head)] = query
            k_part[head] = key
            v_part[head] = value

    def over_chips(step):
        to = lax.rem(chip + step, chips)
        return pltpu.make_async_remote_copy(
            src_ref=gain_chips.at[chip],
            dst_ref=gain_chips.at[chip],
            send_sem=gain_chips_send.at[step - 1],
            recv_sem=gain_chips_recv.at[chip],
            device_id={"seq": 2 * to + core},
            device_id_type=MESH,
        )

    def from_chips(step):
        place = lax.rem(chip + step, chips)
        return pltpu.make_async_remote_copy(
            src_ref=gain_chips.at[place],
            dst_ref=gain_chips.at[place],
            send_sem=gain_chips_send.at[step - 1],
            recv_sem=gain_chips_recv.at[place],
            device_id={"seq": 2 * place + core},
            device_id_type=MESH,
        )

    def over_rows(step):
        return pltpu.make_async_remote_copy(
            src_ref=gain_rows.at[place_z],
            dst_ref=gain_rows.at[place_z],
            send_sem=gain_rows_send.at[step - 1],
            recv_sem=gain_rows_recv.at[place_z],
            device_id={"dp": lax.rem(place_z + step, rows_of)},
            device_id_type=MESH,
        )

    def from_rows(step):
        place = lax.rem(place_z + step, rows_of)
        return pltpu.make_async_remote_copy(
            src_ref=gain_rows.at[place],
            dst_ref=gain_rows.at[place],
            send_sem=gain_rows_send.at[step - 1],
            recv_sem=gain_rows_recv.at[place],
            device_id={"dp": place},
            device_id_type=MESH,
        )

    def each_step(stop, action):
        def turn(step, carried):
            action(step)
            return carried

        lax.fori_loop(1, stop, turn, 0)

    def gain_begin():
        for local in range(half):
            gain_chips[chip, local : local + 1, :] = (
                gain_row[pl.ds(core * half + local, 1), :] + peer_ref[1, local, HD + 1 : HD + 2, :]
            )
        each_step(chips, lambda step: over_chips(step).start())

    def gain_middle():
        each_step(chips, lambda step: from_chips(step).wait_recv())
        total = gain_chips[0]
        for one in range(1, chips):
            total = total + gain_chips[one]
        gain_rows[place_z] = total
        each_step(rows_of, lambda step: over_rows(step).start())

    gain_pass = pltpu.make_async_remote_copy(
        src_ref=gain_far.at[0],
        dst_ref=gain_far.at[1],
        send_sem=gain_far_sem.at[0],
        recv_sem=gain_far_sem.at[1],
        device_id={"seq": peer},
        device_id_type=MESH,
    )

    def gain_end():
        each_step(rows_of, lambda step: from_rows(step).wait_recv())
        total = gain_rows[0]
        for one in range(1, rows_of):
            total = total + gain_rows[one]
        gain_far[0] = total / math.sqrt(blk * seqs * rows_of)
        gain_pass.start()

    late = chips - early
    back = (core == 1, chip < chips - 1, chip > 0, lax.rem(seq + seqs - 2, seqs))

    @pl.when(chip < late)
    def _():
        each_head(masked, 0, half)
        join(1, core == 1, chip > 0)
        gain_begin()
        each_head(masked, half, half)
        gain_middle()

    @pl.when(chip >= late)
    def _():
        join(1, core == 1, chip > 0)
        gain_begin()

    chain(1, *back)

    @pl.when(chip >= late)
    def _():
        each_head(masked, 0, heads)
        gain_middle()

    gain_end()

    def finish(group):
        made = []
        for head in group:
            state = state_ref[1, head]
            leave = leave_ref[head]
            key = k_part[head] + leave * dot(v_ref[:, lanes(head)], state, 1, 1)
            value = v_part[head] + leave * dot(k_ref[:, lanes(head)], state, 1, 0)
            made.append((key.astype(BF16), value.astype(BF16)))
        for head, (key, value) in zip(group, made):
            k_out[0, :, lanes(head)] = key
            v_out[0, :, lanes(head)] = value

    each_head(finish, 0, heads)

    gain_pass.wait_recv()
    for local in range(half):
        gain_out[pl.ds(core * half + local, 1), :] = gain_far[0, local : local + 1, :]
        gain_out[pl.ds(other * half + local, 1), :] = gain_far[1, local : local + 1, :]
    gain_pass.wait_send()
    each_step(chips, lambda step: over_chips(step).wait_send())
    each_step(rows_of, lambda step: over_rows(step).wait_send())
    for share in shares:
        share.wait_send()
    for way, has_next in ((0, chip < chips - 1), (1, chip > 0)):
        exchange(way).wait_send()

        def sent(index, carried, way=way, has_next=has_next):
            @pl.when(has_next)
            def _():
                ahead(way, index, peer).wait_send()

            across(way, index).wait_send()
            return carried

        lax.fori_loop(0, chunks, sent, 0)


def on_device(seqs, teams, rows_of, queries, keys_in, values_in, grad_output, log_decay, lengths, norm_gain):
    tokens, features = queries.shape[1:]
    heads = log_decay.shape[2]
    half = heads // 2
    chunks = half * SPLIT
    whole = jax.ShapeDtypeStruct((1, tokens, features), BF16)
    anywhere = pl.BlockSpec(memory_space=pltpu.HBM)
    vmem = pl.BlockSpec(memory_space=pltpu.VMEM)
    wide = pltpu.VMEM((heads, tokens, HD), F32)
    states = pltpu.VMEM((2, half, HD, HD), F32)
    query_grad, key_grad, value_grad, gain = pl.pallas_call(
        functools.partial(kernel, seqs, teams, rows_of),
        out_shape=(whole, whole, whole, jax.ShapeDtypeStruct((heads, HD), F32)),
        in_specs=[anywhere] * 5 + [pl.BlockSpec(memory_space=pltpu.SMEM), vmem],
        out_specs=[vmem] * 4,
        scratch_shapes=[
            pltpu.VMEM((tokens, features), BF16),
            pltpu.VMEM((tokens, features), BF16),
            pltpu.VMEM((tokens, features), BF16),
            pltpu.VMEM((tokens, features), BF16),
            pltpu.VMEM((heads, tokens), F32),
            pltpu.VMEM((heads, tokens), F32),
            wide,
            pltpu.VMEM((tokens, tokens), F32),
            wide,
            wide,
            pltpu.VMEM((heads, tokens, tokens), F32),
            pltpu.VMEM((heads, tokens, tokens), BF16),
            pltpu.VMEM((heads, tokens, HD), BF16),
            wide,
            pltpu.VMEM((heads, tokens, HD), BF16),
            pltpu.VMEM((tokens, HD), F32),
            pltpu.VMEM((tokens, HD), F32),
            wide,
            wide,
            pltpu.VMEM((2, heads, HD + TAG, HD), F32),
            pltpu.VMEM((2, half, HD + TAG, HD), F32),
            states,
            states,
            states,
            states,
            pltpu.VMEM((2, heads, HD, HD), BF16),
            pltpu.VMEM((16, tokens), F32),
            pltpu.VMEM((teams - 1, 16, tokens), F32),
            pltpu.VMEM((heads, HD), F32),
            pltpu.VMEM((seqs // 2, half, HD), F32),
            pltpu.VMEM((rows_of, half, HD), F32),
            pltpu.VMEM((2, half, HD), F32),
            pltpu.SemaphoreType.DMA((5,)),
            pltpu.SemaphoreType.DMA((2,)),
            pltpu.SemaphoreType.DMA((2,)),
            pltpu.SemaphoreType.DMA((2, chunks)),
            pltpu.SemaphoreType.DMA((2, chunks)),
            pltpu.SemaphoreType.DMA((2, chunks)),
            pltpu.SemaphoreType.DMA((2, chunks)),
            pltpu.SemaphoreType.DMA((teams - 1,)),
            pltpu.SemaphoreType.DMA((teams - 1,)),
            pltpu.SemaphoreType.DMA((seqs // 2 - 1,)),
            pltpu.SemaphoreType.DMA((seqs // 2,)),
            pltpu.SemaphoreType.DMA((rows_of - 1,)),
            pltpu.SemaphoreType.DMA((rows_of,)),
            pltpu.SemaphoreType.DMA((2,)),
        ],
        compiler_params=pltpu.CompilerParams(
            collective_id=0, has_side_effects=True, vmem_limit_bytes=63 * 1024 * 1024
        ),
    )(
        queries,
        keys_in,
        values_in,
        grad_output,
        jnp.swapaxes(log_decay, 1, 2),
        lengths,
        norm_gain.reshape(heads, HD),
    )
    return query_grad, key_grad, value_grad, gain.reshape(features)


def solution(mesh):
    split = P("dp", "seq", "head")
    return jax.shard_map(
        functools.partial(on_device, mesh.shape["seq"], mesh.shape["head"], mesh.shape["dp"]),
        mesh=mesh,
        in_specs=(split, split, split, split, split, P("dp", None), P("head")),
        out_specs=(split, split, split, P("head")),
        check_vma=False,
    )
```

```python
import functools
import math

import jax
import jax.numpy as jnp
from jax import lax
from jax.experimental import pallas as pl
from jax.experimental.pallas import tpu as pltpu
from jax.sharding import PartitionSpec as P

EPSILON = 1e-06
HD = 128
TAG = 8
SPLIT = 2
UNROLL = 4
MESH = pl.DeviceIdType.MESH
EXACT = lax.Precision.HIGHEST
F32 = jnp.float32
BF16 = jnp.bfloat16


def dot(left, right, over_left, over_right, precision=None):
    return lax.dot_general(
        left,
        right,
        (((over_left,), (over_right,)), ((), ())),
        preferred_element_type=F32,
        precision=precision,
    )


def each_head(body, start, count):
    def turn(step, carried):
        body([start + step * UNROLL + one for one in range(UNROLL)])
        return carried

    lax.fori_loop(0, count // UNROLL, turn, 0)


def kernel(
    seqs,
    teams,
    rows_of,
    q_hbm,
    k_hbm,
    v_hbm,
    up_hbm,
    log_hbm,
    lengths,
    gain_in,
    q_out,
    k_out,
    v_out,
    gain_out,
    q_ref,
    k_ref,
    v_ref,
    up_ref,
    log_ref,
    c_row,
    c_col,
    bias_ref,
    enter_ref,
    leave_ref,
    decay_ref,
    weight_ref,
    entered_ref,
    attn_ref,
    grad_ref,
    squares_ref,
    inner_ref,
    k_part,
    v_part,
    own_ref,
    peer_ref,
    step_in,
    carry_ref,
    chain_in,
    chain_out,
    pass_ref,
    far_ref,
    state_ref,
    sums_ref,
    sums_in,
    gain_row,
    gain_chips,
    gain_rows,
    gain_far,
    load_sem,
    pair_send,
    pair_recv,
    step_send,
    step_recv,
    carry_send,
    carry_recv,
    chain_send,
    chain_recv,
    back_send,
    back_recv,
    pass_send,
    pass_recv,
    sums_send,
    sums_recv,
    gain_chips_send,
    gain_chips_recv,
    gain_rows_send,
    gain_rows_recv,
    gain_far_sem,
):
    blk, features = q_ref.shape
    heads = features // HD
    half = heads // 2
    chunks = half * SPLIT
    span = HD // SPLIT
    chips = seqs // 2
    seq = lax.axis_index("seq")
    team = lax.axis_index("head")
    place_z = lax.axis_index("dp")
    core = lax.rem(seq, 2)
    chip = lax.div(seq, 2)
    other = 1 - core
    peer = seq + 1 - 2 * core

    loads = [
        pltpu.make_async_copy(source.at[0], target, load_sem.at[slot])
        for slot, (source, target) in enumerate(
            [(log_hbm, log_ref), (k_hbm, k_ref), (v_hbm, v_ref), (q_hbm, q_ref), (up_hbm, up_ref)]
        )
    ]
    for load in loads:
        load.start()

    barrier = pltpu.get_barrier_semaphore()
    pl.semaphore_signal(barrier, inc=1, device_id={"seq": peer}, device_id_type=MESH)
    for step in range(1, teams):
        pl.semaphore_signal(
            barrier, inc=1, device_id={"head": lax.rem(team + step, teams)}, device_id_type=MESH
        )

    for step in range(1, chips):
        pl.semaphore_signal(
            barrier, inc=1, device_id={"seq": lax.rem(seq + 2 * step, seqs)}, device_id_type=MESH
        )

    def greet(step, carried):
        pl.semaphore_signal(
            barrier, inc=1, device_id={"dp": lax.rem(place_z + step, rows_of)}, device_id_type=MESH
        )
        return carried

    lax.fori_loop(1, rows_of, greet, 0)

    def lanes(head):
        return pl.ds(pl.multiple_of(head * HD, HD), HD)

    row = lax.broadcasted_iota(jnp.int32, (blk, blk), 0)
    col = lax.broadcasted_iota(jnp.int32, (blk, blk), 1)
    triangle = (col <= row).astype(F32)
    places = []
    total = 0
    for one in range(lengths.shape[1] - 1):
        total = total + lengths[0, one]
        place = total - seq * blk
        places.append(jnp.where(place < 0, 2 * blk, place))
    at_row = lax.broadcasted_iota(jnp.int32, (blk, 1), 0)
    at_col = lax.broadcasted_iota(jnp.int32, (1, blk), 1)
    z_row = sum((at_row >= place).astype(jnp.int32) for place in places)
    z_col = sum((at_col >= place).astype(jnp.int32) for place in places)
    z_end = sum(jnp.where(place < blk, 1, 0) for place in places)
    loads[0].wait()
    log = log_ref[...]
    c_all = dot(triangle, log, 1, 1, EXACT)
    tail = c_all[blk - 1 : blk, :]
    leaving = jnp.exp(tail - c_all) * (z_row == z_end).astype(F32)
    carry = jnp.exp(tail) * jnp.where(z_end == 0, 1.0, 0.0)
    for head in range(heads):
        leave_ref[head] = jnp.broadcast_to(leaving[:, head : head + 1], (blk, HD))
        tag = jnp.broadcast_to(carry[:, head : head + 1], (TAG, HD))
        own_ref[0, head, HD : HD + TAG, :] = tag
        own_ref[1, head, HD : HD + TAG, :] = tag

    def block_state(group):
        made = []
        for head in group:
            left = (k_ref[:, lanes(head)].astype(F32) * leave_ref[head]).astype(BF16)
            made.append(dot(left, v_ref[:, lanes(head)], 0, 0))
        for head, value in zip(group, made):
            own_ref[0, head, 0:HD, :] = value

    def exchange(way):
        return pltpu.make_async_remote_copy(
            src_ref=own_ref.at[way, pl.ds(other * half, half)],
            dst_ref=peer_ref.at[way],
            send_sem=pair_send.at[way],
            recv_sem=pair_recv.at[way],
            device_id={"seq": peer},
            device_id_type=MESH,
        )

    def beside(way, chips_on):
        return lax.rem(seq + 2 * (chips_on if way == 0 else -chips_on) + seqs, seqs)

    def piece(way, index):
        start = pl.multiple_of(lax.rem(index, SPLIT) * span, span)
        return way, lax.div(index, SPLIT), pl.ds(start, span)

    def hand_on(way, index):
        return pltpu.make_async_remote_copy(
            src_ref=chain_out.at[piece(way, index)],
            dst_ref=step_in.at[piece(way, index)],
            send_sem=step_send.at[way, index],
            recv_sem=step_recv.at[way, index],
            device_id={"seq": beside(way, 1)},
            device_id_type=MESH,
        )

    def carried_on(way):
        return pltpu.make_async_remote_copy(
            src_ref=carry_ref.at[way, 0],
            dst_ref=carry_ref.at[way, 1],
            send_sem=carry_send.at[way],
            recv_sem=carry_recv.at[way],
            device_id={"seq": beside(way, 1)},
            device_id_type=MESH,
        )

    def ahead(way, index):
        return pltpu.make_async_remote_copy(
            src_ref=chain_out.at[piece(way, index)],
            dst_ref=chain_in.at[piece(way, index)],
            send_sem=chain_send.at[way, index],
            recv_sem=chain_recv.at[way, index],
            device_id={"seq": beside(way, 2)},
            device_id_type=MESH,
        )

    def back(way, index):
        return pltpu.make_async_remote_copy(
            src_ref=chain_in.at[piece(way, index)],
            dst_ref=chain_in.at[piece(way, index)],
            send_sem=back_send.at[way, index],
            recv_sem=back_recv.at[way, index],
            device_id={"seq": beside(way, -1)},
            device_id_type=MESH,
        )

    def across(way, index):
        return pltpu.make_async_remote_copy(
            src_ref=pass_ref.at[piece(way, index)],
            dst_ref=far_ref.at[piece(way, index)],
            send_sem=pass_send.at[way, index],
            recv_sem=pass_recv.at[way, index],
            device_id={"seq": peer},
            device_id_type=MESH,
        )

    def each_chunk(body):
        def turn(index, carried):
            body(index)
            return carried

        lax.fori_loop(0, chunks, turn, 0)

    ways = []
    for way in (0, 1):
        order = chip if way == 0 else chips - 1 - chip
        second = lax.rem(order, 2) == 1
        inner = order >= 2
        ways.append(
            (
                core == way,
                second,
                jnp.logical_not(second),
                inner,
                jnp.logical_and(second, inner),
                jnp.logical_and(jnp.logical_not(second), inner),
                jnp.logical_and(second, order < chips - 1),
                jnp.logical_and(second, order == 1),
            )
        )

    def join(way):
        lead, second, opening = ways[way][:3]
        exchange(way).wait_recv()

        def joined(local, carried):
            mine = own_ref[way, core * half + local, 0:HD, :]
            theirs = peer_ref[way, local, 0:HD, :]
            my_carry = own_ref[way, core * half + local, HD : HD + 1, :]
            their_carry = peer_ref[way, local, HD : HD + 1, :]
            carry_ref[way, 0, pl.ds(local, 1), :] = my_carry * their_carry
            chain_out[way, local] = jnp.where(
                lead, their_carry * mine + theirs, my_carry * theirs + mine
            )
            return carried

        lax.fori_loop(0, half, joined, 0)

        @pl.when(opening)
        def _():
            each_chunk(lambda index: hand_on(way, index).start())
            carried_on(way).start()
            step_in[way] = jnp.zeros(step_in.shape[1:], F32)
            carry_ref[way, 1] = jnp.ones(carry_ref.shape[2:], F32)

    def pair_up(way):
        second, onward, inner = ways[way][1], ways[way][6], ways[way][3]

        @pl.when(second)
        def _():
            carried_on(way).wait_recv()

            def body(index):
                at = piece(way, index)
                hand_on(way, index).wait_recv()
                chain_out[at] = carry_ref[way, 0, pl.ds(at[1], 1), :] * step_in[at] + chain_out[at]

                @pl.when(jnp.logical_and(onward, jnp.logical_not(inner)))
                def _():
                    ahead(way, index).start()

            each_chunk(body)

        @pl.when(jnp.logical_not(inner))
        def _():
            chain_in[way] = jnp.zeros(chain_in.shape[1:], F32)

    def chain(way):
        lead, second, opening, inner, second_inner, opening_inner, onward, seed = ways[way]

        def body(index):
            at = piece(way, index)
            local, rows = at[1:]

            @pl.when(second_inner)
            def _():
                ahead(way, index).wait_recv()

                @pl.when(onward)
                def _():
                    both = carry_ref[way, 0, pl.ds(local, 1), :] * carry_ref[way, 1, pl.ds(local, 1), :]
                    chain_out[at] = both * chain_in[at] + chain_out[at]
                    ahead(way, index).start()

                back(way, index).start()

            @pl.when(opening_inner)
            def _():
                back(way, index).wait_recv()

            my_carry = own_ref[way, core * half + local, HD : HD + 1, :]
            their_carry = peer_ref[way, local, HD : HD + 1, :]
            state = carry_ref[way, 1, pl.ds(local, 1), :] * chain_in[at] + step_in[at]
            mine = own_ref[way, core * half + local, rows, :]
            theirs = peer_ref[way, local, rows, :]
            middle = jnp.where(lead, my_carry * state + mine, their_carry * state + theirs)
            pass_ref[at] = jnp.where(lead, middle, state)
            across(way, index).start()
            state_ref[way, core * half + local, rows, :] = jnp.where(lead, state, middle).astype(BF16)

        each_chunk(body)

        def land(index):
            at = piece(way, index)
            across(way, index).wait_recv()
            state_ref[way, other * half + at[1], at[2], :] = far_ref[at].astype(BF16)

        each_chunk(land)

    loads[1].wait()
    loads[2].wait()
    each_head(block_state, other * half, half)
    pl.semaphore_wait(barrier, 1 + teams - 1 + chips - 1 + rows_of - 1)
    exchange(0).start()
    each_head(block_state, core * half, half)

    c_row[...] = dot(log, triangle, 1, 1, EXACT)
    entering = jnp.exp(c_all) * (z_row == 0).astype(F32)
    for head in range(heads):
        enter_ref[head] = jnp.broadcast_to(entering[:, head : head + 1], (blk, HD))
        c_col[head] = jnp.broadcast_to(c_all[:, head : head + 1], (blk, HD))
    bias_ref[...] = jnp.where((z_row == z_col) & (col <= row), 0.0, -1e30)
    loads[3].wait()
    loads[4].wait()

    def near(group):
        made = []
        for head in group:
            query = q_ref[:, lanes(head)]
            scores = dot(query, k_ref[:, lanes(head)], 1, 1)
            start = jnp.broadcast_to(c_col[head][:, 0:1], (blk, blk))
            decay = jnp.exp(start - c_row[pl.ds(head, 1), :] + bias_ref[...])
            weight = (scores * decay).astype(BF16)
            entered = (query.astype(F32) * enter_ref[head]).astype(BF16)
            made.append((decay, weight, entered, dot(weight, v_ref[:, lanes(head)], 1, 0)))
        for head, (decay, weight, entered, value) in zip(group, made):
            decay_ref[head] = decay
            weight_ref[head] = weight
            entered_ref[head] = entered
            attn_ref[head] = value

    join(0)

    @pl.when(ways[0][3])
    def _():
        each_head(near, 0, heads)

    pair_up(0)
    chain(0)

    @pl.when(jnp.logical_not(ways[0][3]))
    def _():
        each_head(near, 0, heads)

    squares_ref[...] = jnp.zeros_like(squares_ref)
    inner_ref[...] = jnp.zeros_like(inner_ref)

    def attend(group):
        squares, inner = squares_ref[...], inner_ref[...]
        made = []
        for head in group:
            attn = attn_ref[head] + dot(entered_ref[head], state_ref[0, head], 1, 0)
            scaled = up_ref[:, lanes(head)].astype(F32) * gain_in[pl.ds(head, 1), :]
            squares = squares + attn * attn
            inner = inner + scaled * attn
            made.append(attn)
        for head, attn in zip(group, made):
            attn_ref[head] = attn
        squares_ref[...] = squares
        inner_ref[...] = inner

    each_head(attend, 0, heads)
    ones = jnp.ones((8, HD), F32)
    sums_ref[0:8, :] = dot(ones, squares_ref[...], 1, 1, EXACT)
    sums_ref[8:16, :] = dot(ones, inner_ref[...], 1, 1, EXACT)
    shares = [
        pltpu.make_async_remote_copy(
            src_ref=sums_ref,
            dst_ref=sums_in.at[step - 1],
            send_sem=sums_send.at[step - 1],
            recv_sem=sums_recv.at[step - 1],
            device_id={"head": lax.rem(team + step, teams)},
            device_id_type=MESH,
        )
        for step in range(1, teams)
    ]
    for share in shares:
        share.start()
    for share in shares:
        share.wait_recv()
    sums = sums_ref[...]
    for step in range(1, teams):
        sums = sums + sums_in[step - 1]
    width = features * teams
    chosen = lax.broadcasted_iota(jnp.int32, (8, HD), 0)
    chosen = jnp.where(chosen == 0, 1.0, 0.0).astype(F32)
    squares = dot(sums[0:8, :], chosen, 0, 0, EXACT)
    inner = dot(sums[8:16, :], chosen, 0, 0, EXACT)
    recip = lax.rsqrt(squares / width + EPSILON)
    squares_ref[...] = recip
    inner_ref[...] = recip * recip * recip * inner / width

    def gradient(group):
        recip, coef = squares_ref[...], inner_ref[...]
        made = []
        for head in group:
            attn = attn_ref[head]
            upstream = up_ref[:, lanes(head)].astype(F32)
            scaled = upstream * gain_in[pl.ds(head, 1), :]
            grad = (recip * scaled - coef * attn).astype(BF16)
            part = jnp.sum(upstream * attn * recip, axis=0, keepdims=True)
            made.append((grad, part, dot(entered_ref[head], grad, 0, 0)))
        for head, (grad, part, value) in zip(group, made):
            grad_ref[head] = grad
            gain_row[pl.ds(head, 1), :] = part
            own_ref[1, head, HD + 1 : HD + 2, :] = part
            own_ref[1, head, 0:HD, :] = value

    each_head(gradient, other * half, half)
    exchange(1).start()
    each_head(gradient, core * half, half)

    def masked(group):
        made = []
        for head in group:
            grad = grad_ref[head]
            raw = dot(grad, v_ref[:, lanes(head)], 1, 1)
            mask = (raw * decay_ref[head]).astype(BF16)
            query = dot(mask, k_ref[:, lanes(head)], 1, 0)
            query = query + enter_ref[head] * dot(grad, state_ref[0, head], 1, 1)
            made.append(
                (
                    query.astype(BF16),
                    dot(mask, q_ref[:, lanes(head)], 0, 0),
                    dot(weight_ref[head], grad, 0, 0),
                )
            )
        for head, (query, key, value) in zip(group, made):
            q_out[0, :, lanes(head)] = query
            k_part[head] = key
            v_part[head] = value

    def over_chips(step):
        to = lax.rem(chip + step, chips)
        return pltpu.make_async_remote_copy(
            src_ref=gain_chips.at[chip],
            dst_ref=gain_chips.at[chip],
            send_sem=gain_chips_send.at[step - 1],
            recv_sem=gain_chips_recv.at[chip],
            device_id={"seq": 2 * to + core},
            device_id_type=MESH,
        )

    def from_chips(step):
        place = lax.rem(chip + step, chips)
        return pltpu.make_async_remote_copy(
            src_ref=gain_chips.at[place],
            dst_ref=gain_chips.at[place],
            send_sem=gain_chips_send.at[step - 1],
            recv_sem=gain_chips_recv.at[place],
            device_id={"seq": 2 * place + core},
            device_id_type=MESH,
        )

    def over_rows(step):
        return pltpu.make_async_remote_copy(
            src_ref=gain_rows.at[place_z],
            dst_ref=gain_rows.at[place_z],
            send_sem=gain_rows_send.at[step - 1],
            recv_sem=gain_rows_recv.at[place_z],
            device_id={"dp": lax.rem(place_z + step, rows_of)},
            device_id_type=MESH,
        )

    def from_rows(step):
        place = lax.rem(place_z + step, rows_of)
        return pltpu.make_async_remote_copy(
            src_ref=gain_rows.at[place],
            dst_ref=gain_rows.at[place],
            send_sem=gain_rows_send.at[step - 1],
            recv_sem=gain_rows_recv.at[place],
            device_id={"dp": place},
            device_id_type=MESH,
        )

    def each_step(stop, action):
        def turn(step, carried):
            action(step)
            return carried

        lax.fori_loop(1, stop, turn, 0)

    def gain_begin():
        for local in range(half):
            gain_chips[chip, local : local + 1, :] = (
                gain_row[pl.ds(core * half + local, 1), :] + peer_ref[1, local, HD + 1 : HD + 2, :]
            )
        each_step(chips, lambda step: over_chips(step).start())

    def gain_middle():
        each_step(chips, lambda step: from_chips(step).wait_recv())
        total = gain_chips[0]
        for one in range(1, chips):
            total = total + gain_chips[one]
        gain_rows[place_z] = total
        each_step(rows_of, lambda step: over_rows(step).start())

    gain_pass = pltpu.make_async_remote_copy(
        src_ref=gain_far.at[0],
        dst_ref=gain_far.at[1],
        send_sem=gain_far_sem.at[0],
        recv_sem=gain_far_sem.at[1],
        device_id={"seq": peer},
        device_id_type=MESH,
    )

    def gain_end():
        each_step(rows_of, lambda step: from_rows(step).wait_recv())
        total = gain_rows[0]
        for one in range(1, rows_of):
            total = total + gain_rows[one]
        gain_far[0] = total / math.sqrt(blk * seqs * rows_of)
        gain_pass.start()

    far_on = chips - 1 - chip >= 4

    @pl.when(ways[1][3])
    def _():
        each_head(masked, 0, half)

    join(1)
    gain_begin()

    @pl.when(ways[1][3])
    def _():
        each_head(masked, half, half)

    @pl.when(far_on)
    def _():
        gain_middle()

    pair_up(1)
    chain(1)

    @pl.when(jnp.logical_not(ways[1][3]))
    def _():
        each_head(masked, 0, heads)

    @pl.when(jnp.logical_not(far_on))
    def _():
        gain_middle()

    gain_end()

    def finish(group):
        made = []
        for head in group:
            state = state_ref[1, head]
            leave = leave_ref[head]
            key = k_part[head] + leave * dot(v_ref[:, lanes(head)], state, 1, 1)
            value = v_part[head] + leave * dot(k_ref[:, lanes(head)], state, 1, 0)
            made.append((key.astype(BF16), value.astype(BF16)))
        for head, (key, value) in zip(group, made):
            k_out[0, :, lanes(head)] = key
            v_out[0, :, lanes(head)] = value

    each_head(finish, 0, heads)

    gain_pass.wait_recv()
    for local in range(half):
        gain_out[pl.ds(core * half + local, 1), :] = gain_far[0, local : local + 1, :]
        gain_out[pl.ds(other * half + local, 1), :] = gain_far[1, local : local + 1, :]
    gain_pass.wait_send()
    each_step(chips, lambda step: over_chips(step).wait_send())
    each_step(rows_of, lambda step: over_rows(step).wait_send())
    for share in shares:
        share.wait_send()
    for way in (0, 1):
        exchange(way).wait_send()
        opening, second_inner, onward = ways[way][2], ways[way][4], ways[way][6]

        @pl.when(opening)
        def _(way=way):
            carried_on(way).wait_send()
            each_chunk(lambda index: hand_on(way, index).wait_send())

        @pl.when(onward)
        def _(way=way):
            each_chunk(lambda index: ahead(way, index).wait_send())

        @pl.when(second_inner)
        def _(way=way):
            each_chunk(lambda index: back(way, index).wait_send())

        each_chunk(lambda index, way=way: across(way, index).wait_send())


def deliver(*refs):
    count = len(refs) // 2
    for one in range(count):
        refs[count + one][...] = refs[one][...]


def on_device(seqs, teams, rows_of, queries, keys_in, values_in, grad_output, log_decay, lengths, norm_gain):
    tokens, features = queries.shape[1:]
    heads = log_decay.shape[2]
    half = heads // 2
    chunks = half * SPLIT
    whole = jax.ShapeDtypeStruct((1, tokens, features), BF16)
    anywhere = pl.BlockSpec(memory_space=pltpu.HBM)
    vmem = pl.BlockSpec(memory_space=pltpu.VMEM)
    wide = pltpu.VMEM((heads, tokens, HD), F32)
    states = pltpu.VMEM((2, half, HD, HD), F32)
    query_grad, key_grad, value_grad, gain = pl.pallas_call(
        functools.partial(kernel, seqs, teams, rows_of),
        out_shape=(whole, whole, whole, jax.ShapeDtypeStruct((heads, HD), F32)),
        in_specs=[anywhere] * 5 + [pl.BlockSpec(memory_space=pltpu.SMEM), vmem],
        out_specs=[vmem] * 4,
        scratch_shapes=[
            pltpu.VMEM((tokens, features), BF16),
            pltpu.VMEM((tokens, features), BF16),
            pltpu.VMEM((tokens, features), BF16),
            pltpu.VMEM((tokens, features), BF16),
            pltpu.VMEM((heads, tokens), F32),
            pltpu.VMEM((heads, tokens), F32),
            wide,
            pltpu.VMEM((tokens, tokens), F32),
            wide,
            wide,
            pltpu.VMEM((heads, tokens, tokens), F32),
            pltpu.VMEM((heads, tokens, tokens), BF16),
            pltpu.VMEM((heads, tokens, HD), BF16),
            wide,
            pltpu.VMEM((heads, tokens, HD), BF16),
            pltpu.VMEM((tokens, HD), F32),
            pltpu.VMEM((tokens, HD), F32),
            wide,
            wide,
            pltpu.VMEM((2, heads, HD + TAG, HD), F32),
            pltpu.VMEM((2, half, HD + TAG, HD), F32),
            states,
            pltpu.VMEM((2, 2, half, HD), F32),
            states,
            states,
            states,
            states,
            pltpu.VMEM((2, heads, HD, HD), BF16),
            pltpu.VMEM((16, tokens), F32),
            pltpu.VMEM((max(teams - 1, 1), 16, tokens), F32),
            pltpu.VMEM((heads, HD), F32),
            pltpu.VMEM((seqs // 2, half, HD), F32),
            pltpu.VMEM((rows_of, half, HD), F32),
            pltpu.VMEM((2, half, HD), F32),
            pltpu.SemaphoreType.DMA((5,)),
            pltpu.SemaphoreType.DMA((2,)),
            pltpu.SemaphoreType.DMA((2,)),
            pltpu.SemaphoreType.DMA((2, chunks)),
            pltpu.SemaphoreType.DMA((2, chunks)),
            pltpu.SemaphoreType.DMA((2,)),
            pltpu.SemaphoreType.DMA((2,)),
            pltpu.SemaphoreType.DMA((2, chunks)),
            pltpu.SemaphoreType.DMA((2, chunks)),
            pltpu.SemaphoreType.DMA((2, chunks)),
            pltpu.SemaphoreType.DMA((2, chunks)),
            pltpu.SemaphoreType.DMA((2, chunks)),
            pltpu.SemaphoreType.DMA((2, chunks)),
            pltpu.SemaphoreType.DMA((max(teams - 1, 1),)),
            pltpu.SemaphoreType.DMA((max(teams - 1, 1),)),
            pltpu.SemaphoreType.DMA((max(seqs // 2 - 1, 1),)),
            pltpu.SemaphoreType.DMA((seqs // 2,)),
            pltpu.SemaphoreType.DMA((max(rows_of - 1, 1),)),
            pltpu.SemaphoreType.DMA((rows_of,)),
            pltpu.SemaphoreType.DMA((2,)),
        ],
        compiler_params=pltpu.CompilerParams(
            collective_id=0, has_side_effects=True, vmem_limit_bytes=63 * 1024 * 1024
        ),
    )(
        queries,
        keys_in,
        values_in,
        grad_output,
        jnp.swapaxes(log_decay, 1, 2),
        lengths,
        norm_gain.reshape(heads, HD),
    )
    made = (query_grad, key_grad, value_grad, gain)
    any_space = pl.BlockSpec(memory_space=pltpu.VMEM)
    query_grad, key_grad, value_grad, gain = pl.pallas_call(
        deliver,
        out_shape=tuple(jax.ShapeDtypeStruct(one.shape, one.dtype) for one in made),
        in_specs=[any_space] * 4,
        out_specs=[any_space] * 4,
    )(*made)
    return query_grad, key_grad, value_grad, gain.reshape(features)


def solution(mesh):
    split = P("dp", "seq", "head")
    return jax.shard_map(
        functools.partial(on_device, mesh.shape["seq"], mesh.shape["head"], mesh.shape["dp"]),
        mesh=mesh,
        in_specs=(split, split, split, split, split, P("dp", None), P("head")),
        out_specs=(split, split, split, P("head")),
        check_vma=False,
    )
```

```python
import functools
import math

import jax
import jax.numpy as jnp
from jax import lax
from jax.experimental import pallas as pl
from jax.experimental.pallas import tpu as pltpu
from jax.sharding import PartitionSpec as P

EPSILON = 1e-06
HD = 128
TAG = 8
SPLIT = 2
UNROLL = 4
REACH = 4
MESH = pl.DeviceIdType.MESH
EXACT = lax.Precision.HIGHEST
F32 = jnp.float32
BF16 = jnp.bfloat16


def dot(left, right, over_left, over_right, precision=None):
    return lax.dot_general(
        left,
        right,
        (((over_left,), (over_right,)), ((), ())),
        preferred_element_type=F32,
        precision=precision,
    )


def each_head(body, start, count):
    def turn(step, carried):
        body([start + step * UNROLL + one for one in range(UNROLL)])
        return carried

    lax.fori_loop(0, count // UNROLL, turn, 0)


def kernel(
    seqs,
    teams,
    rows_of,
    q_hbm,
    k_hbm,
    v_hbm,
    up_hbm,
    log_hbm,
    lengths,
    gain_in,
    q_out,
    k_out,
    v_out,
    gain_out,
    q_ref,
    k_ref,
    v_ref,
    up_ref,
    log_ref,
    c_row,
    c_col,
    bias_ref,
    enter_ref,
    leave_ref,
    decay_ref,
    weight_ref,
    entered_ref,
    attn_ref,
    grad_ref,
    squares_ref,
    inner_ref,
    k_part,
    v_part,
    own_ref,
    peer_ref,
    step_in,
    carry_ref,
    chain_in,
    chain_out,
    pass_ref,
    far_ref,
    state_ref,
    sums_ref,
    sums_in,
    gain_row,
    gain_chips,
    gain_rows,
    gain_far,
    load_sem,
    pair_send,
    pair_recv,
    step_send,
    step_recv,
    carry_send,
    carry_recv,
    chain_send,
    chain_recv,
    back_send,
    back_recv,
    pass_send,
    pass_recv,
    sums_send,
    sums_recv,
    gain_chips_send,
    gain_chips_recv,
    gain_rows_send,
    gain_rows_recv,
    gain_far_sem,
    told_sem,
):
    blk, features = q_ref.shape
    heads = features // HD
    half = heads // 2
    chunks = half * SPLIT
    span = HD // SPLIT
    chips = seqs // 2
    seq = lax.axis_index("seq")
    team = lax.axis_index("head")
    place_z = lax.axis_index("dp")
    core = lax.rem(seq, 2)
    chip = lax.div(seq, 2)
    other = 1 - core
    peer = seq + 1 - 2 * core

    loads = [
        pltpu.make_async_copy(source.at[0], target, load_sem.at[slot])
        for slot, (source, target) in enumerate(
            [(log_hbm, log_ref), (k_hbm, k_ref), (v_hbm, v_ref), (q_hbm, q_ref), (up_hbm, up_ref)]
        )
    ]
    for load in loads:
        load.start()

    barrier = pltpu.get_barrier_semaphore()
    pl.semaphore_signal(barrier, inc=1, device_id={"seq": peer}, device_id_type=MESH)
    for step in range(1, teams):
        pl.semaphore_signal(
            barrier, inc=1, device_id={"head": lax.rem(team + step, teams)}, device_id_type=MESH
        )

    for step in range(1, chips):
        pl.semaphore_signal(
            barrier, inc=1, device_id={"seq": lax.rem(seq + 2 * step, seqs)}, device_id_type=MESH
        )

    def each_along_z(distance, action):
        for side, place in enumerate((place_z - distance, place_z + distance)):

            @pl.when(jnp.logical_and(place >= 0, place < rows_of))
            def _(side=side, place=place):
                action(side, place)

    close = min(REACH, rows_of - 1)
    for distance in range(1, close + 1):
        each_along_z(
            distance,
            lambda side, place: pl.semaphore_signal(
                barrier, inc=1, device_id={"dp": place}, device_id_type=MESH
            ),
        )
    greeted = 1 + teams - 1 + chips - 1
    for distance in range(1, close + 1):
        greeted = greeted + jnp.where(place_z >= distance, 1, 0)
        greeted = greeted + jnp.where(place_z + distance < rows_of, 1, 0)

    def tell(turn):
        each_along_z(
            REACH << turn,
            lambda side, place: pl.semaphore_signal(
                told_sem.at[turn, side], inc=1, device_id={"dp": place}, device_id_type=MESH
            ),
        )

    def hear(turn):
        each_along_z(
            REACH << turn, lambda side, place: pl.semaphore_wait(told_sem.at[turn, 1 - side], 1)
        )

    turns = 0
    while REACH << turns < rows_of:
        turns += 1

    def lanes(head):
        return pl.ds(pl.multiple_of(head * HD, HD), HD)

    row = lax.broadcasted_iota(jnp.int32, (blk, blk), 0)
    col = lax.broadcasted_iota(jnp.int32, (blk, blk), 1)
    triangle = (col <= row).astype(F32)
    places = []
    total = 0
    for one in range(lengths.shape[1] - 1):
        total = total + lengths[0, one]
        place = total - seq * blk
        places.append(jnp.where(place < 0, 2 * blk, place))
    at_row = lax.broadcasted_iota(jnp.int32, (blk, 1), 0)
    at_col = lax.broadcasted_iota(jnp.int32, (1, blk), 1)
    z_row = sum((at_row >= place).astype(jnp.int32) for place in places)
    z_col = sum((at_col >= place).astype(jnp.int32) for place in places)
    z_end = sum(jnp.where(place < blk, 1, 0) for place in places)
    loads[0].wait()
    log = log_ref[...]
    c_all = dot(triangle, log, 1, 1, EXACT)
    tail = c_all[blk - 1 : blk, :]
    leaving = jnp.exp(tail - c_all) * (z_row == z_end).astype(F32)
    carry = jnp.exp(tail) * jnp.where(z_end == 0, 1.0, 0.0)
    for head in range(heads):
        leave_ref[head] = jnp.broadcast_to(leaving[:, head : head + 1], (blk, HD))
        tag = jnp.broadcast_to(carry[:, head : head + 1], (TAG, HD))
        own_ref[0, head, HD : HD + TAG, :] = tag
        own_ref[1, head, HD : HD + TAG, :] = tag

    def block_state(group):
        made = []
        for head in group:
            left = (k_ref[:, lanes(head)].astype(F32) * leave_ref[head]).astype(BF16)
            made.append(dot(left, v_ref[:, lanes(head)], 0, 0))
        for head, value in zip(group, made):
            own_ref[0, head, 0:HD, :] = value

    def exchange(way):
        return pltpu.make_async_remote_copy(
            src_ref=own_ref.at[way, pl.ds(other * half, half)],
            dst_ref=peer_ref.at[way],
            send_sem=pair_send.at[way],
            recv_sem=pair_recv.at[way],
            device_id={"seq": peer},
            device_id_type=MESH,
        )

    def beside(way, chips_on):
        return lax.rem(seq + 2 * (chips_on if way == 0 else -chips_on) + seqs, seqs)

    def piece(way, index):
        start = pl.multiple_of(lax.rem(index, SPLIT) * span, span)
        return way, lax.div(index, SPLIT), pl.ds(start, span)

    def hand_on(way, index):
        return pltpu.make_async_remote_copy(
            src_ref=chain_out.at[piece(way, index)],
            dst_ref=step_in.at[piece(way, index)],
            send_sem=step_send.at[way, index],
            recv_sem=step_recv.at[way, index],
            device_id={"seq": beside(way, 1)},
            device_id_type=MESH,
        )

    def carried_on(way):
        return pltpu.make_async_remote_copy(
            src_ref=carry_ref.at[way, 0],
            dst_ref=carry_ref.at[way, 1],
            send_sem=carry_send.at[way],
            recv_sem=carry_recv.at[way],
            device_id={"seq": beside(way, 1)},
            device_id_type=MESH,
        )

    def ahead(way, index):
        return pltpu.make_async_remote_copy(
            src_ref=chain_out.at[piece(way, index)],
            dst_ref=chain_in.at[piece(way, index)],
            send_sem=chain_send.at[way, index],
            recv_sem=chain_recv.at[way, index],
            device_id={"seq": beside(way, 2)},
            device_id_type=MESH,
        )

    def back(way, index):
        return pltpu.make_async_remote_copy(
            src_ref=chain_in.at[piece(way, index)],
            dst_ref=chain_in.at[piece(way, index)],
            send_sem=back_send.at[way, index],
            recv_sem=back_recv.at[way, index],
            device_id={"seq": beside(way, -1)},
            device_id_type=MESH,
        )

    def across(way, index):
        return pltpu.make_async_remote_copy(
            src_ref=pass_ref.at[piece(way, index)],
            dst_ref=far_ref.at[piece(way, index)],
            send_sem=pass_send.at[way, index],
            recv_sem=pass_recv.at[way, index],
            device_id={"seq": peer},
            device_id_type=MESH,
        )

    def each_chunk(body):
        def turn(index, carried):
            body(index)
            return carried

        lax.fori_loop(0, chunks, turn, 0)

    ways = []
    for way in (0, 1):
        order = chip if way == 0 else chips - 1 - chip
        second = lax.rem(order, 2) == 1
        inner = order >= 2
        ways.append(
            (
                core == way,
                second,
                jnp.logical_not(second),
                inner,
                jnp.logical_and(second, inner),
                jnp.logical_and(jnp.logical_not(second), inner),
                jnp.logical_and(second, order < chips - 1),
                jnp.logical_and(second, order == 1),
            )
        )

    def join(way):
        lead, second, opening = ways[way][:3]
        exchange(way).wait_recv()

        def joined(local, carried):
            mine = own_ref[way, core * half + local, 0:HD, :]
            theirs = peer_ref[way, local, 0:HD, :]
            my_carry = own_ref[way, core * half + local, HD : HD + 1, :]
            their_carry = peer_ref[way, local, HD : HD + 1, :]
            carry_ref[way, 0, pl.ds(local, 1), :] = my_carry * their_carry
            chain_out[way, local] = jnp.where(
                lead, their_carry * mine + theirs, my_carry * theirs + mine
            )
            return carried

        lax.fori_loop(0, half, joined, 0)

        @pl.when(opening)
        def _():
            each_chunk(lambda index: hand_on(way, index).start())
            carried_on(way).start()
            step_in[way] = jnp.zeros(step_in.shape[1:], F32)
            carry_ref[way, 1] = jnp.ones(carry_ref.shape[2:], F32)

    def pair_up(way):
        second, onward, inner = ways[way][1], ways[way][6], ways[way][3]

        @pl.when(second)
        def _():
            carried_on(way).wait_recv()

            def body(index):
                at = piece(way, index)
                hand_on(way, index).wait_recv()
                chain_out[at] = carry_ref[way, 0, pl.ds(at[1], 1), :] * step_in[at] + chain_out[at]

                @pl.when(jnp.logical_and(onward, jnp.logical_not(inner)))
                def _():
                    ahead(way, index).start()

            each_chunk(body)

        @pl.when(jnp.logical_not(inner))
        def _():
            chain_in[way] = jnp.zeros(chain_in.shape[1:], F32)

    def chain(way):
        lead, second, opening, inner, second_inner, opening_inner, onward, seed = ways[way]

        def body(index):
            at = piece(way, index)
            local, rows = at[1:]

            @pl.when(second_inner)
            def _():
                ahead(way, index).wait_recv()

                @pl.when(onward)
                def _():
                    both = carry_ref[way, 0, pl.ds(local, 1), :] * carry_ref[way, 1, pl.ds(local, 1), :]
                    chain_out[at] = both * chain_in[at] + chain_out[at]
                    ahead(way, index).start()

                back(way, index).start()

            @pl.when(opening_inner)
            def _():
                back(way, index).wait_recv()

            my_carry = own_ref[way, core * half + local, HD : HD + 1, :]
            their_carry = peer_ref[way, local, HD : HD + 1, :]
            state = carry_ref[way, 1, pl.ds(local, 1), :] * chain_in[at] + step_in[at]
            mine = own_ref[way, core * half + local, rows, :]
            theirs = peer_ref[way, local, rows, :]
            middle = jnp.where(lead, my_carry * state + mine, their_carry * state + theirs)
            pass_ref[at] = jnp.where(lead, middle, state)
            across(way, index).start()
            state_ref[way, core * half + local, rows, :] = jnp.where(lead, state, middle).astype(BF16)

        each_chunk(body)

        def land(index):
            at = piece(way, index)
            across(way, index).wait_recv()
            state_ref[way, other * half + at[1], at[2], :] = far_ref[at].astype(BF16)

        each_chunk(land)

    loads[1].wait()
    loads[2].wait()
    each_head(block_state, other * half, half)
    pl.semaphore_wait(barrier, greeted)
    exchange(0).start()
    if turns:
        tell(0)
    each_head(block_state, core * half, half)

    c_row[...] = dot(log, triangle, 1, 1, EXACT)
    entering = jnp.exp(c_all) * (z_row == 0).astype(F32)
    for head in range(heads):
        enter_ref[head] = jnp.broadcast_to(entering[:, head : head + 1], (blk, HD))
        c_col[head] = jnp.broadcast_to(c_all[:, head : head + 1], (blk, HD))
    bias_ref[...] = jnp.where((z_row == z_col) & (col <= row), 0.0, -1e30)
    loads[3].wait()
    loads[4].wait()

    def near(group):
        made = []
        for head in group:
            query = q_ref[:, lanes(head)]
            scores = dot(query, k_ref[:, lanes(head)], 1, 1)
            start = jnp.broadcast_to(c_col[head][:, 0:1], (blk, blk))
            decay = jnp.exp(start - c_row[pl.ds(head, 1), :] + bias_ref[...])
            weight = (scores * decay).astype(BF16)
            entered = (query.astype(F32) * enter_ref[head]).astype(BF16)
            made.append((decay, weight, entered, dot(weight, v_ref[:, lanes(head)], 1, 0)))
        for head, (decay, weight, entered, value) in zip(group, made):
            decay_ref[head] = decay
            weight_ref[head] = weight
            entered_ref[head] = entered
            attn_ref[head] = value

    join(0)

    @pl.when(ways[0][3])
    def _():
        each_head(near, 0, heads)

    pair_up(0)
    chain(0)

    @pl.when(jnp.logical_not(ways[0][3]))
    def _():
        each_head(near, 0, heads)

    for turn in range(1, turns):
        hear(turn - 1)
        tell(turn)

    squares_ref[...] = jnp.zeros_like(squares_ref)
    inner_ref[...] = jnp.zeros_like(inner_ref)

    def attend(group):
        squares, inner = squares_ref[...], inner_ref[...]
        made = []
        for head in group:
            attn = attn_ref[head] + dot(entered_ref[head], state_ref[0, head], 1, 0)
            scaled = up_ref[:, lanes(head)].astype(F32) * gain_in[pl.ds(head, 1), :]
            squares = squares + attn * attn
            inner = inner + scaled * attn
            made.append(attn)
        for head, attn in zip(group, made):
            attn_ref[head] = attn
        squares_ref[...] = squares
        inner_ref[...] = inner

    each_head(attend, 0, heads)
    ones = jnp.ones((8, HD), F32)
    sums_ref[0:8, :] = dot(ones, squares_ref[...], 1, 1, EXACT)
    sums_ref[8:16, :] = dot(ones, inner_ref[...], 1, 1, EXACT)
    shares = [
        pltpu.make_async_remote_copy(
            src_ref=sums_ref,
            dst_ref=sums_in.at[step - 1],
            send_sem=sums_send.at[step - 1],
            recv_sem=sums_recv.at[step - 1],
            device_id={"head": lax.rem(team + step, teams)},
            device_id_type=MESH,
        )
        for step in range(1, teams)
    ]
    for share in shares:
        share.start()
    for share in shares:
        share.wait_recv()
    sums = sums_ref[...]
    for step in range(1, teams):
        sums = sums + sums_in[step - 1]
    width = features * teams
    chosen = lax.broadcasted_iota(jnp.int32, (8, HD), 0)
    chosen = jnp.where(chosen == 0, 1.0, 0.0).astype(F32)
    squares = dot(sums[0:8, :], chosen, 0, 0, EXACT)
    inner = dot(sums[8:16, :], chosen, 0, 0, EXACT)
    recip = lax.rsqrt(squares / width + EPSILON)
    squares_ref[...] = recip
    inner_ref[...] = recip * recip * recip * inner / width

    def gradient(group):
        recip, coef = squares_ref[...], inner_ref[...]
        made = []
        for head in group:
            attn = attn_ref[head]
            upstream = up_ref[:, lanes(head)].astype(F32)
            scaled = upstream * gain_in[pl.ds(head, 1), :]
            grad = (recip * scaled - coef * attn).astype(BF16)
            part = jnp.sum(upstream * attn * recip, axis=0, keepdims=True)
            made.append((grad, part, dot(entered_ref[head], grad, 0, 0)))
        for head, (grad, part, value) in zip(group, made):
            grad_ref[head] = grad
            gain_row[pl.ds(head, 1), :] = part
            own_ref[1, head, HD + 1 : HD + 2, :] = part
            own_ref[1, head, 0:HD, :] = value

    each_head(gradient, other * half, half)
    exchange(1).start()
    each_head(gradient, core * half, half)

    def masked(group):
        made = []
        for head in group:
            grad = grad_ref[head]
            raw = dot(grad, v_ref[:, lanes(head)], 1, 1)
            mask = (raw * decay_ref[head]).astype(BF16)
            query = dot(mask, k_ref[:, lanes(head)], 1, 0)
            query = query + enter_ref[head] * dot(grad, state_ref[0, head], 1, 1)
            made.append(
                (
                    query.astype(BF16),
                    dot(mask, q_ref[:, lanes(head)], 0, 0),
                    dot(weight_ref[head], grad, 0, 0),
                )
            )
        for head, (query, key, value) in zip(group, made):
            q_out[0, :, lanes(head)] = query
            k_part[head] = key
            v_part[head] = value

    def over_chips(step):
        to = lax.rem(chip + step, chips)
        return pltpu.make_async_remote_copy(
            src_ref=gain_chips.at[chip],
            dst_ref=gain_chips.at[chip],
            send_sem=gain_chips_send.at[step - 1],
            recv_sem=gain_chips_recv.at[chip],
            device_id={"seq": 2 * to + core},
            device_id_type=MESH,
        )

    def from_chips(step):
        place = lax.rem(chip + step, chips)
        return pltpu.make_async_remote_copy(
            src_ref=gain_chips.at[place],
            dst_ref=gain_chips.at[place],
            send_sem=gain_chips_send.at[step - 1],
            recv_sem=gain_chips_recv.at[place],
            device_id={"seq": 2 * place + core},
            device_id_type=MESH,
        )

    def over_rows(step):
        return pltpu.make_async_remote_copy(
            src_ref=gain_rows.at[place_z],
            dst_ref=gain_rows.at[place_z],
            send_sem=gain_rows_send.at[step - 1],
            recv_sem=gain_rows_recv.at[place_z],
            device_id={"dp": lax.rem(place_z + step, rows_of)},
            device_id_type=MESH,
        )

    def from_rows(step):
        place = lax.rem(place_z + step, rows_of)
        return pltpu.make_async_remote_copy(
            src_ref=gain_rows.at[place],
            dst_ref=gain_rows.at[place],
            send_sem=gain_rows_send.at[step - 1],
            recv_sem=gain_rows_recv.at[place],
            device_id={"dp": place},
            device_id_type=MESH,
        )

    def each_step(stop, action):
        def turn(step, carried):
            action(step)
            return carried

        lax.fori_loop(1, stop, turn, 0)

    def gain_begin():
        for local in range(half):
            gain_chips[chip, local : local + 1, :] = (
                gain_row[pl.ds(core * half + local, 1), :] + peer_ref[1, local, HD + 1 : HD + 2, :]
            )
        each_step(chips, lambda step: over_chips(step).start())

    def gain_middle():
        if turns:
            hear(turns - 1)
        each_step(chips, lambda step: from_chips(step).wait_recv())
        total = gain_chips[0]
        for one in range(1, chips):
            total = total + gain_chips[one]
        gain_rows[place_z] = total
        each_step(rows_of, lambda step: over_rows(step).start())

    gain_pass = pltpu.make_async_remote_copy(
        src_ref=gain_far.at[0],
        dst_ref=gain_far.at[1],
        send_sem=gain_far_sem.at[0],
        recv_sem=gain_far_sem.at[1],
        device_id={"seq": peer},
        device_id_type=MESH,
    )

    def gain_end():
        each_step(rows_of, lambda step: from_rows(step).wait_recv())
        total = gain_rows[0]
        for one in range(1, rows_of):
            total = total + gain_rows[one]
        gain_far[0] = total / math.sqrt(blk * seqs * rows_of)
        gain_pass.start()

    far_on = chips - 1 - chip >= 4

    @pl.when(ways[1][3])
    def _():
        each_head(masked, 0, half)

    join(1)
    gain_begin()

    @pl.when(ways[1][3])
    def _():
        each_head(masked, half, half)

    @pl.when(far_on)
    def _():
        gain_middle()

    pair_up(1)
    chain(1)

    @pl.when(jnp.logical_not(ways[1][3]))
    def _():
        each_head(masked, 0, heads)

    @pl.when(jnp.logical_not(far_on))
    def _():
        gain_middle()

    gain_end()

    def finish(group):
        made = []
        for head in group:
            state = state_ref[1, head]
            leave = leave_ref[head]
            key = k_part[head] + leave * dot(v_ref[:, lanes(head)], state, 1, 1)
            value = v_part[head] + leave * dot(k_ref[:, lanes(head)], state, 1, 0)
            made.append((key.astype(BF16), value.astype(BF16)))
        for head, (key, value) in zip(group, made):
            k_out[0, :, lanes(head)] = key
            v_out[0, :, lanes(head)] = value

    each_head(finish, 0, heads)

    gain_pass.wait_recv()
    for local in range(half):
        gain_out[pl.ds(core * half + local, 1), :] = gain_far[0, local : local + 1, :]
        gain_out[pl.ds(other * half + local, 1), :] = gain_far[1, local : local + 1, :]
    gain_pass.wait_send()
    each_step(chips, lambda step: over_chips(step).wait_send())
    each_step(rows_of, lambda step: over_rows(step).wait_send())
    for share in shares:
        share.wait_send()
    for way in (0, 1):
        exchange(way).wait_send()
        opening, second_inner, onward = ways[way][2], ways[way][4], ways[way][6]

        @pl.when(opening)
        def _(way=way):
            carried_on(way).wait_send()
            each_chunk(lambda index: hand_on(way, index).wait_send())

        @pl.when(onward)
        def _(way=way):
            each_chunk(lambda index: ahead(way, index).wait_send())

        @pl.when(second_inner)
        def _(way=way):
            each_chunk(lambda index: back(way, index).wait_send())

        each_chunk(lambda index, way=way: across(way, index).wait_send())


def deliver(*refs):
    count = len(refs) // 2
    for one in range(count):
        refs[count + one][...] = refs[one][...]


def on_device(seqs, teams, rows_of, queries, keys_in, values_in, grad_output, log_decay, lengths, norm_gain):
    tokens, features = queries.shape[1:]
    heads = log_decay.shape[2]
    half = heads // 2
    chunks = half * SPLIT
    whole = jax.ShapeDtypeStruct((1, tokens, features), BF16)
    anywhere = pl.BlockSpec(memory_space=pltpu.HBM)
    vmem = pl.BlockSpec(memory_space=pltpu.VMEM)
    wide = pltpu.VMEM((heads, tokens, HD), F32)
    states = pltpu.VMEM((2, half, HD, HD), F32)
    query_grad, key_grad, value_grad, gain = pl.pallas_call(
        functools.partial(kernel, seqs, teams, rows_of),
        out_shape=(whole, whole, whole, jax.ShapeDtypeStruct((heads, HD), F32)),
        in_specs=[anywhere] * 5 + [pl.BlockSpec(memory_space=pltpu.SMEM), vmem],
        out_specs=[vmem] * 4,
        scratch_shapes=[
            pltpu.VMEM((tokens, features), BF16),
            pltpu.VMEM((tokens, features), BF16),
            pltpu.VMEM((tokens, features), BF16),
            pltpu.VMEM((tokens, features), BF16),
            pltpu.VMEM((heads, tokens), F32),
            pltpu.VMEM((heads, tokens), F32),
            wide,
            pltpu.VMEM((tokens, tokens), F32),
            wide,
            wide,
            pltpu.VMEM((heads, tokens, tokens), F32),
            pltpu.VMEM((heads, tokens, tokens), BF16),
            pltpu.VMEM((heads, tokens, HD), BF16),
            wide,
            pltpu.VMEM((heads, tokens, HD), BF16),
            pltpu.VMEM((tokens, HD), F32),
            pltpu.VMEM((tokens, HD), F32),
            wide,
            wide,
            pltpu.VMEM((2, heads, HD + TAG, HD), F32),
            pltpu.VMEM((2, half, HD + TAG, HD), F32),
            states,
            pltpu.VMEM((2, 2, half, HD), F32),
            states,
            states,
            states,
            states,
            pltpu.VMEM((2, heads, HD, HD), BF16),
            pltpu.VMEM((16, tokens), F32),
            pltpu.VMEM((max(teams - 1, 1), 16, tokens), F32),
            pltpu.VMEM((heads, HD), F32),
            pltpu.VMEM((seqs // 2, half, HD), F32),
            pltpu.VMEM((rows_of, half, HD), F32),
            pltpu.VMEM((2, half, HD), F32),
            pltpu.SemaphoreType.DMA((5,)),
            pltpu.SemaphoreType.DMA((2,)),
            pltpu.SemaphoreType.DMA((2,)),
            pltpu.SemaphoreType.DMA((2, chunks)),
            pltpu.SemaphoreType.DMA((2, chunks)),
            pltpu.SemaphoreType.DMA((2,)),
            pltpu.SemaphoreType.DMA((2,)),
            pltpu.SemaphoreType.DMA((2, chunks)),
            pltpu.SemaphoreType.DMA((2, chunks)),
            pltpu.SemaphoreType.DMA((2, chunks)),
            pltpu.SemaphoreType.DMA((2, chunks)),
            pltpu.SemaphoreType.DMA((2, chunks)),
            pltpu.SemaphoreType.DMA((2, chunks)),
            pltpu.SemaphoreType.DMA((max(teams - 1, 1),)),
            pltpu.SemaphoreType.DMA((max(teams - 1, 1),)),
            pltpu.SemaphoreType.DMA((max(seqs // 2 - 1, 1),)),
            pltpu.SemaphoreType.DMA((seqs // 2,)),
            pltpu.SemaphoreType.DMA((max(rows_of - 1, 1),)),
            pltpu.SemaphoreType.DMA((rows_of,)),
            pltpu.SemaphoreType.DMA((2,)),
            pltpu.SemaphoreType.REGULAR((8, 2)),
        ],
        compiler_params=pltpu.CompilerParams(
            collective_id=0, has_side_effects=True, vmem_limit_bytes=63 * 1024 * 1024
        ),
    )(
        queries,
        keys_in,
        values_in,
        grad_output,
        jnp.swapaxes(log_decay, 1, 2),
        lengths,
        norm_gain.reshape(heads, HD),
    )
    made = (query_grad, key_grad, value_grad, gain)
    any_space = pl.BlockSpec(memory_space=pltpu.VMEM)
    query_grad, key_grad, value_grad, gain = pl.pallas_call(
        deliver,
        out_shape=tuple(jax.ShapeDtypeStruct(one.shape, one.dtype) for one in made),
        in_specs=[any_space] * 4,
        out_specs=[any_space] * 4,
    )(*made)
    return query_grad, key_grad, value_grad, gain.reshape(features)


def solution(mesh):
    split = P("dp", "seq", "head")
    return jax.shard_map(
        functools.partial(on_device, mesh.shape["seq"], mesh.shape["head"], mesh.shape["dp"]),
        mesh=mesh,
        in_specs=(split, split, split, split, split, P("dp", None), P("head")),
        out_specs=(split, split, split, P("head")),
        check_vma=False,
    )
```

```python
import functools
import math

import jax
import jax.numpy as jnp
from jax import lax
from jax.experimental import pallas as pl
from jax.experimental.pallas import tpu as pltpu
from jax.sharding import PartitionSpec as P

EPSILON = 1e-06
HD = 128
TAG = 8
SPLIT = 2
UNROLL = 4
REACH = 4
MESH = pl.DeviceIdType.MESH
EXACT = lax.Precision.HIGHEST
F32 = jnp.float32
BF16 = jnp.bfloat16


def dot(left, right, over_left, over_right, precision=None):
    return lax.dot_general(
        left,
        right,
        (((over_left,), (over_right,)), ((), ())),
        preferred_element_type=F32,
        precision=precision,
    )


def each_head(body, start, count):
    def turn(step, carried):
        body([start + step * UNROLL + one for one in range(UNROLL)])
        return carried

    lax.fori_loop(0, count // UNROLL, turn, 0)


def kernel(
    seqs,
    teams,
    rows_of,
    q_hbm,
    k_hbm,
    v_hbm,
    up_hbm,
    log_hbm,
    lengths,
    gain_in,
    q_out,
    k_out,
    v_out,
    gain_out,
    q_ref,
    k_ref,
    v_ref,
    up_ref,
    log_ref,
    c_row,
    c_col,
    bias_ref,
    enter_ref,
    leave_ref,
    decay_ref,
    weight_ref,
    entered_ref,
    attn_ref,
    grad_ref,
    squares_ref,
    inner_ref,
    k_part,
    v_part,
    own_ref,
    peer_ref,
    step_in,
    carry_ref,
    chain_in,
    chain_out,
    pass_ref,
    far_ref,
    state_ref,
    sums_ref,
    sums_in,
    gain_row,
    gain_chips,
    gain_rows,
    gain_far,
    load_sem,
    pair_send,
    pair_recv,
    step_send,
    step_recv,
    carry_send,
    carry_recv,
    chain_send,
    chain_recv,
    back_send,
    back_recv,
    pass_send,
    pass_recv,
    sums_send,
    sums_recv,
    gain_chips_send,
    gain_chips_recv,
    gain_rows_send,
    gain_rows_recv,
    gain_far_sem,
    told_sem,
):
    blk, features = q_ref.shape
    heads = features // HD
    half = heads // 2
    chunks = half * SPLIT
    span = HD // SPLIT
    chips = seqs // 2
    seq = lax.axis_index("seq")
    team = lax.axis_index("head")
    place_z = lax.axis_index("dp")
    core = lax.rem(seq, 2)
    chip = lax.div(seq, 2)
    other = 1 - core
    peer = seq + 1 - 2 * core

    loads = [
        pltpu.make_async_copy(source.at[0], target, load_sem.at[slot])
        for slot, (source, target) in enumerate(
            [(log_hbm, log_ref), (k_hbm, k_ref), (v_hbm, v_ref), (q_hbm, q_ref), (up_hbm, up_ref)]
        )
    ]
    for load in loads:
        load.start()

    barrier = pltpu.get_barrier_semaphore()
    pl.semaphore_signal(barrier, inc=1, device_id={"seq": peer}, device_id_type=MESH)
    for step in range(1, teams):
        pl.semaphore_signal(
            barrier, inc=1, device_id={"head": lax.rem(team + step, teams)}, device_id_type=MESH
        )

    for step in range(1, chips):
        pl.semaphore_signal(
            barrier, inc=1, device_id={"seq": lax.rem(seq + 2 * step, seqs)}, device_id_type=MESH
        )

    def each_along_z(distance, action):
        for side, place in enumerate((place_z - distance, place_z + distance)):

            @pl.when(jnp.logical_and(place >= 0, place < rows_of))
            def _(side=side, place=place):
                action(side, place)

    close = min(REACH, rows_of - 1)
    for distance in range(1, close + 1):
        each_along_z(
            distance,
            lambda side, place: pl.semaphore_signal(
                barrier, inc=1, device_id={"dp": place}, device_id_type=MESH
            ),
        )
    greeted = 1 + teams - 1 + chips - 1
    for distance in range(1, close + 1):
        greeted = greeted + jnp.where(place_z >= distance, 1, 0)
        greeted = greeted + jnp.where(place_z + distance < rows_of, 1, 0)

    def tell(turn):
        each_along_z(
            REACH << turn,
            lambda side, place: pl.semaphore_signal(
                told_sem.at[turn, side], inc=1, device_id={"dp": place}, device_id_type=MESH
            ),
        )

    def hear(turn):
        each_along_z(
            REACH << turn, lambda side, place: pl.semaphore_wait(told_sem.at[turn, 1 - side], 1)
        )

    turns = 0
    while REACH << turns < rows_of:
        turns += 1

    def lanes(head):
        return pl.ds(pl.multiple_of(head * HD, HD), HD)

    row = lax.broadcasted_iota(jnp.int32, (blk, blk), 0)
    col = lax.broadcasted_iota(jnp.int32, (blk, blk), 1)
    triangle = (col <= row).astype(F32)
    places = []
    total = 0
    for one in range(lengths.shape[1] - 1):
        total = total + lengths[0, one]
        place = total - seq * blk
        places.append(jnp.where(place < 0, 2 * blk, place))
    at_row = lax.broadcasted_iota(jnp.int32, (blk, 1), 0)
    at_col = lax.broadcasted_iota(jnp.int32, (1, blk), 1)
    z_row = sum((at_row >= place).astype(jnp.int32) for place in places)
    z_col = sum((at_col >= place).astype(jnp.int32) for place in places)
    z_end = sum(jnp.where(place < blk, 1, 0) for place in places)
    loads[0].wait()
    log = log_ref[...]
    c_all = dot(triangle, log, 1, 1, EXACT)
    tail = c_all[blk - 1 : blk, :]
    leaving = jnp.exp(tail - c_all) * (z_row == z_end).astype(F32)
    carry = jnp.exp(tail) * jnp.where(z_end == 0, 1.0, 0.0)
    for head in range(heads):
        leave_ref[head] = jnp.broadcast_to(leaving[:, head : head + 1], (blk, HD))
        tag = jnp.broadcast_to(carry[:, head : head + 1], (TAG, HD))
        own_ref[0, head, HD : HD + TAG, :] = tag
        own_ref[1, head, HD : HD + TAG, :] = tag

    def block_state(group):
        made = []
        for head in group:
            left = (k_ref[:, lanes(head)].astype(F32) * leave_ref[head]).astype(BF16)
            made.append(dot(left, v_ref[:, lanes(head)], 0, 0))
        for head, value in zip(group, made):
            own_ref[0, head, 0:HD, :] = value

    def exchange(way):
        return pltpu.make_async_remote_copy(
            src_ref=own_ref.at[way, pl.ds(other * half, half)],
            dst_ref=peer_ref.at[way],
            send_sem=pair_send.at[way],
            recv_sem=pair_recv.at[way],
            device_id={"seq": peer},
            device_id_type=MESH,
        )

    def beside(way, chips_on):
        return lax.rem(seq + 2 * (chips_on if way == 0 else -chips_on) + seqs, seqs)

    def piece(way, index):
        start = pl.multiple_of(lax.rem(index, SPLIT) * span, span)
        return way, lax.div(index, SPLIT), pl.ds(start, span)

    def hand_on(way, index):
        return pltpu.make_async_remote_copy(
            src_ref=chain_out.at[piece(way, index)],
            dst_ref=step_in.at[piece(way, index)],
            send_sem=step_send.at[way, index],
            recv_sem=step_recv.at[way, index],
            device_id={"seq": beside(way, 1)},
            device_id_type=MESH,
        )

    def carried_on(way):
        return pltpu.make_async_remote_copy(
            src_ref=carry_ref.at[way, 0],
            dst_ref=carry_ref.at[way, 1],
            send_sem=carry_send.at[way],
            recv_sem=carry_recv.at[way],
            device_id={"seq": beside(way, 1)},
            device_id_type=MESH,
        )

    def ahead(way, index):
        return pltpu.make_async_remote_copy(
            src_ref=chain_out.at[piece(way, index)],
            dst_ref=chain_in.at[piece(way, index)],
            send_sem=chain_send.at[way, index],
            recv_sem=chain_recv.at[way, index],
            device_id={"seq": beside(way, 2)},
            device_id_type=MESH,
        )

    def back(way, index):
        return pltpu.make_async_remote_copy(
            src_ref=chain_in.at[piece(way, index)],
            dst_ref=chain_in.at[piece(way, index)],
            send_sem=back_send.at[way, index],
            recv_sem=back_recv.at[way, index],
            device_id={"seq": beside(way, -1)},
            device_id_type=MESH,
        )

    def across(way, index):
        return pltpu.make_async_remote_copy(
            src_ref=pass_ref.at[piece(way, index)],
            dst_ref=far_ref.at[piece(way, index)],
            send_sem=pass_send.at[way, index],
            recv_sem=pass_recv.at[way, index],
            device_id={"seq": peer},
            device_id_type=MESH,
        )

    def each_chunk(body):
        def turn(index, carried):
            body(index)
            return carried

        lax.fori_loop(0, chunks, turn, 0)

    ways = []
    for way in (0, 1):
        order = chip if way == 0 else chips - 1 - chip
        second = lax.rem(order, 2) == 1
        inner = order >= 2
        ways.append(
            (
                core == way,
                second,
                jnp.logical_not(second),
                inner,
                jnp.logical_and(second, inner),
                jnp.logical_and(jnp.logical_not(second), inner),
                jnp.logical_and(second, order < chips - 1),
                jnp.logical_and(second, order == 1),
            )
        )

    def join(way):
        lead, second, opening = ways[way][:3]
        exchange(way).wait_recv()

        def joined(local, carried):
            mine = own_ref[way, core * half + local, 0:HD, :]
            theirs = peer_ref[way, local, 0:HD, :]
            my_carry = own_ref[way, core * half + local, HD : HD + 1, :]
            their_carry = peer_ref[way, local, HD : HD + 1, :]
            carry_ref[way, 0, pl.ds(local, 1), :] = my_carry * their_carry
            chain_out[way, local] = jnp.where(
                lead, their_carry * mine + theirs, my_carry * theirs + mine
            )
            return carried

        lax.fori_loop(0, half, joined, 0)

        @pl.when(opening)
        def _():
            each_chunk(lambda index: hand_on(way, index).start())
            carried_on(way).start()
            step_in[way] = jnp.zeros(step_in.shape[1:], F32)
            carry_ref[way, 1] = jnp.ones(carry_ref.shape[2:], F32)

    def pair_up(way):
        second, onward, inner = ways[way][1], ways[way][6], ways[way][3]

        @pl.when(second)
        def _():
            carried_on(way).wait_recv()

            def body(index):
                at = piece(way, index)
                hand_on(way, index).wait_recv()
                chain_out[at] = carry_ref[way, 0, pl.ds(at[1], 1), :] * step_in[at] + chain_out[at]

                @pl.when(jnp.logical_and(onward, jnp.logical_not(inner)))
                def _():
                    ahead(way, index).start()

            each_chunk(body)

        @pl.when(jnp.logical_not(inner))
        def _():
            chain_in[way] = jnp.zeros(chain_in.shape[1:], F32)

    def chain(way):
        lead, second, opening, inner, second_inner, opening_inner, onward, seed = ways[way]

        def body(index):
            at = piece(way, index)
            local, rows = at[1:]

            @pl.when(second_inner)
            def _():
                ahead(way, index).wait_recv()

                @pl.when(onward)
                def _():
                    both = carry_ref[way, 0, pl.ds(local, 1), :] * carry_ref[way, 1, pl.ds(local, 1), :]
                    chain_out[at] = both * chain_in[at] + chain_out[at]
                    ahead(way, index).start()

                back(way, index).start()

            @pl.when(opening_inner)
            def _():
                back(way, index).wait_recv()

            my_carry = own_ref[way, core * half + local, HD : HD + 1, :]
            their_carry = peer_ref[way, local, HD : HD + 1, :]
            state = carry_ref[way, 1, pl.ds(local, 1), :] * chain_in[at] + step_in[at]
            mine = own_ref[way, core * half + local, rows, :]
            theirs = peer_ref[way, local, rows, :]
            middle = jnp.where(lead, my_carry * state + mine, their_carry * state + theirs)
            pass_ref[at] = jnp.where(lead, middle, state)
            across(way, index).start()
            state_ref[way, core * half + local, rows, :] = jnp.where(lead, state, middle).astype(BF16)

        each_chunk(body)

        def land(index):
            at = piece(way, index)
            across(way, index).wait_recv()
            state_ref[way, other * half + at[1], at[2], :] = far_ref[at].astype(BF16)

        each_chunk(land)

    loads[1].wait()
    loads[2].wait()
    each_head(block_state, other * half, half)
    pl.semaphore_wait(barrier, greeted)
    exchange(0).start()
    if turns:
        tell(0)
    each_head(block_state, core * half, half)

    c_row[...] = dot(log, triangle, 1, 1, EXACT)
    entering = jnp.exp(c_all) * (z_row == 0).astype(F32)
    for head in range(heads):
        enter_ref[head] = jnp.broadcast_to(entering[:, head : head + 1], (blk, HD))
        c_col[head] = jnp.broadcast_to(c_all[:, head : head + 1], (blk, HD))
    bias_ref[...] = jnp.where((z_row == z_col) & (col <= row), 0.0, -1e30)
    loads[3].wait()
    loads[4].wait()

    def near(group):
        made = []
        for head in group:
            query = q_ref[:, lanes(head)]
            scores = dot(query, k_ref[:, lanes(head)], 1, 1)
            start = jnp.broadcast_to(c_col[head][:, 0:1], (blk, blk))
            decay = jnp.exp(start - c_row[pl.ds(head, 1), :] + bias_ref[...])
            weight = (scores * decay).astype(BF16)
            entered = (query.astype(F32) * enter_ref[head]).astype(BF16)
            made.append((decay, weight, entered, dot(weight, v_ref[:, lanes(head)], 1, 0)))
        for head, (decay, weight, entered, value) in zip(group, made):
            decay_ref[head] = decay
            weight_ref[head] = weight
            entered_ref[head] = entered
            attn_ref[head] = value

    join(0)

    @pl.when(ways[0][3])
    def _():
        each_head(near, 0, heads)

    pair_up(0)
    chain(0)

    @pl.when(jnp.logical_not(ways[0][3]))
    def _():
        each_head(near, 0, heads)

    for turn in range(1, turns):
        hear(turn - 1)
        tell(turn)

    squares_ref[...] = jnp.zeros_like(squares_ref)
    inner_ref[...] = jnp.zeros_like(inner_ref)

    def attend(group):
        squares, inner = squares_ref[...], inner_ref[...]
        made = []
        for head in group:
            attn = attn_ref[head] + dot(entered_ref[head], state_ref[0, head], 1, 0)
            scaled = up_ref[:, lanes(head)].astype(F32) * gain_in[pl.ds(head, 1), :]
            squares = squares + attn * attn
            inner = inner + scaled * attn
            made.append(attn)
        for head, attn in zip(group, made):
            attn_ref[head] = attn
        squares_ref[...] = squares
        inner_ref[...] = inner

    each_head(attend, 0, heads)
    ones = jnp.ones((8, HD), F32)
    sums_ref[0:8, :] = dot(ones, squares_ref[...], 1, 1, EXACT)
    sums_ref[8:16, :] = dot(ones, inner_ref[...], 1, 1, EXACT)
    shares = [
        pltpu.make_async_remote_copy(
            src_ref=sums_ref,
            dst_ref=sums_in.at[step - 1],
            send_sem=sums_send.at[step - 1],
            recv_sem=sums_recv.at[step - 1],
            device_id={"head": lax.rem(team + step, teams)},
            device_id_type=MESH,
        )
        for step in range(1, teams)
    ]
    for share in shares:
        share.start()
    for share in shares:
        share.wait_recv()
    sums = sums_ref[...]
    for step in range(1, teams):
        sums = sums + sums_in[step - 1]
    width = features * teams
    chosen = lax.broadcasted_iota(jnp.int32, (8, HD), 0)
    chosen = jnp.where(chosen == 0, 1.0, 0.0).astype(F32)
    squares = dot(sums[0:8, :], chosen, 0, 0, EXACT)
    inner = dot(sums[8:16, :], chosen, 0, 0, EXACT)
    recip = lax.rsqrt(squares / width + EPSILON)
    squares_ref[...] = recip
    inner_ref[...] = recip * recip * recip * inner / width

    def gradient(group):
        recip, coef = squares_ref[...], inner_ref[...]
        made = []
        for head in group:
            attn = attn_ref[head]
            upstream = up_ref[:, lanes(head)].astype(F32)
            scaled = upstream * gain_in[pl.ds(head, 1), :]
            grad = (recip * scaled - coef * attn).astype(BF16)
            part = jnp.sum(upstream * attn * recip, axis=0, keepdims=True)
            made.append((grad, part, dot(entered_ref[head], grad, 0, 0)))
        for head, (grad, part, value) in zip(group, made):
            grad_ref[head] = grad
            gain_row[pl.ds(head, 1), :] = part
            own_ref[1, head, HD + 1 : HD + 2, :] = part
            own_ref[1, head, 0:HD, :] = value

    each_head(gradient, other * half, half)
    exchange(1).start()
    each_head(gradient, core * half, half)

    def masked(group):
        made = []
        for head in group:
            grad = grad_ref[head]
            raw = dot(grad, v_ref[:, lanes(head)], 1, 1)
            mask = (raw * decay_ref[head]).astype(BF16)
            query = dot(mask, k_ref[:, lanes(head)], 1, 0)
            query = query + enter_ref[head] * dot(grad, state_ref[0, head], 1, 1)
            made.append(
                (
                    query.astype(BF16),
                    dot(mask, q_ref[:, lanes(head)], 0, 0),
                    dot(weight_ref[head], grad, 0, 0),
                )
            )
        for head, (query, key, value) in zip(group, made):
            q_out[0, :, lanes(head)] = query
            k_part[head] = key
            v_part[head] = value

    def over_chips(step):
        to = lax.rem(chip + step, chips)
        return pltpu.make_async_remote_copy(
            src_ref=gain_chips.at[chip],
            dst_ref=gain_chips.at[chip],
            send_sem=gain_chips_send.at[step - 1],
            recv_sem=gain_chips_recv.at[chip],
            device_id={"seq": 2 * to + core},
            device_id_type=MESH,
        )

    def from_chips(step):
        place = lax.rem(chip + step, chips)
        return pltpu.make_async_remote_copy(
            src_ref=gain_chips.at[place],
            dst_ref=gain_chips.at[place],
            send_sem=gain_chips_send.at[step - 1],
            recv_sem=gain_chips_recv.at[place],
            device_id={"seq": 2 * place + core},
            device_id_type=MESH,
        )

    def over_rows(step):
        return pltpu.make_async_remote_copy(
            src_ref=gain_rows.at[place_z],
            dst_ref=gain_rows.at[place_z],
            send_sem=gain_rows_send.at[step - 1],
            recv_sem=gain_rows_recv.at[place_z],
            device_id={"dp": lax.rem(place_z + step, rows_of)},
            device_id_type=MESH,
        )

    def from_rows(step):
        place = lax.rem(place_z + step, rows_of)
        return pltpu.make_async_remote_copy(
            src_ref=gain_rows.at[place],
            dst_ref=gain_rows.at[place],
            send_sem=gain_rows_send.at[step - 1],
            recv_sem=gain_rows_recv.at[place],
            device_id={"dp": place},
            device_id_type=MESH,
        )

    def each_step(stop, action):
        def turn(step, carried):
            action(step)
            return carried

        lax.fori_loop(1, stop, turn, 0)

    def gain_begin():
        for local in range(half):
            gain_chips[chip, local : local + 1, :] = (
                gain_row[pl.ds(core * half + local, 1), :] + peer_ref[1, local, HD + 1 : HD + 2, :]
            )
        each_step(chips, lambda step: over_chips(step).start())

    def gain_middle():
        if turns:
            hear(turns - 1)
        each_step(chips, lambda step: from_chips(step).wait_recv())
        total = gain_chips[0]
        for one in range(1, chips):
            total = total + gain_chips[one]
        gain_rows[place_z] = total
        each_step(rows_of, lambda step: over_rows(step).start())

    gain_pass = pltpu.make_async_remote_copy(
        src_ref=gain_far.at[0],
        dst_ref=gain_far.at[1],
        send_sem=gain_far_sem.at[0],
        recv_sem=gain_far_sem.at[1],
        device_id={"seq": peer},
        device_id_type=MESH,
    )

    def gain_end():
        each_step(rows_of, lambda step: from_rows(step).wait_recv())
        total = gain_rows[0]
        for one in range(1, rows_of):
            total = total + gain_rows[one]
        gain_far[0] = total / math.sqrt(blk * seqs * rows_of)
        gain_pass.start()

    far_on = ways[1][3]

    @pl.when(far_on)
    def _():
        each_head(masked, 0, half)

    join(1)
    gain_begin()

    @pl.when(far_on)
    def _():
        each_head(masked, half, half)

    pair_up(1)

    @pl.when(far_on)
    def _():
        gain_middle()

    chain(1)

    @pl.when(jnp.logical_not(far_on))
    def _():
        gain_middle()
        each_head(masked, 0, heads)

    last = chips - 1 - chip >= 4

    @pl.when(last)
    def _():
        gain_end()

    def finish(group):
        made = []
        for head in group:
            state = state_ref[1, head]
            leave = leave_ref[head]
            key = k_part[head] + leave * dot(v_ref[:, lanes(head)], state, 1, 1)
            value = v_part[head] + leave * dot(k_ref[:, lanes(head)], state, 1, 0)
            made.append((key.astype(BF16), value.astype(BF16)))
        for head, (key, value) in zip(group, made):
            k_out[0, :, lanes(head)] = key
            v_out[0, :, lanes(head)] = value

    each_head(finish, 0, heads)

    @pl.when(jnp.logical_not(last))
    def _():
        gain_end()


    gain_pass.wait_recv()
    for local in range(half):
        gain_out[pl.ds(core * half + local, 1), :] = gain_far[0, local : local + 1, :]
        gain_out[pl.ds(other * half + local, 1), :] = gain_far[1, local : local + 1, :]
    gain_pass.wait_send()
    each_step(chips, lambda step: over_chips(step).wait_send())
    each_step(rows_of, lambda step: over_rows(step).wait_send())
    for share in shares:
        share.wait_send()
    for way in (0, 1):
        exchange(way).wait_send()
        opening, second_inner, onward = ways[way][2], ways[way][4], ways[way][6]

        @pl.when(opening)
        def _(way=way):
            carried_on(way).wait_send()
            each_chunk(lambda index: hand_on(way, index).wait_send())

        @pl.when(onward)
        def _(way=way):
            each_chunk(lambda index: ahead(way, index).wait_send())

        @pl.when(second_inner)
        def _(way=way):
            each_chunk(lambda index: back(way, index).wait_send())

        each_chunk(lambda index, way=way: across(way, index).wait_send())


def deliver(*refs):
    count = len(refs) // 2
    for one in range(count):
        refs[count + one][...] = refs[one][...]


def on_device(seqs, teams, rows_of, queries, keys_in, values_in, grad_output, log_decay, lengths, norm_gain):
    tokens, features = queries.shape[1:]
    heads = log_decay.shape[2]
    half = heads // 2
    chunks = half * SPLIT
    whole = jax.ShapeDtypeStruct((1, tokens, features), BF16)
    anywhere = pl.BlockSpec(memory_space=pltpu.HBM)
    vmem = pl.BlockSpec(memory_space=pltpu.VMEM)
    wide = pltpu.VMEM((heads, tokens, HD), F32)
    states = pltpu.VMEM((2, half, HD, HD), F32)
    query_grad, key_grad, value_grad, gain = pl.pallas_call(
        functools.partial(kernel, seqs, teams, rows_of),
        out_shape=(whole, whole, whole, jax.ShapeDtypeStruct((heads, HD), F32)),
        in_specs=[anywhere] * 5 + [pl.BlockSpec(memory_space=pltpu.SMEM), vmem],
        out_specs=[vmem] * 4,
        scratch_shapes=[
            pltpu.VMEM((tokens, features), BF16),
            pltpu.VMEM((tokens, features), BF16),
            pltpu.VMEM((tokens, features), BF16),
            pltpu.VMEM((tokens, features), BF16),
            pltpu.VMEM((heads, tokens), F32),
            pltpu.VMEM((heads, tokens), F32),
            wide,
            pltpu.VMEM((tokens, tokens), F32),
            wide,
            wide,
            pltpu.VMEM((heads, tokens, tokens), F32),
            pltpu.VMEM((heads, tokens, tokens), BF16),
            pltpu.VMEM((heads, tokens, HD), BF16),
            wide,
            pltpu.VMEM((heads, tokens, HD), BF16),
            pltpu.VMEM((tokens, HD), F32),
            pltpu.VMEM((tokens, HD), F32),
            wide,
            wide,
            pltpu.VMEM((2, heads, HD + TAG, HD), F32),
            pltpu.VMEM((2, half, HD + TAG, HD), F32),
            states,
            pltpu.VMEM((2, 2, half, HD), F32),
            states,
            states,
            states,
            states,
            pltpu.VMEM((2, heads, HD, HD), BF16),
            pltpu.VMEM((16, tokens), F32),
            pltpu.VMEM((max(teams - 1, 1), 16, tokens), F32),
            pltpu.VMEM((heads, HD), F32),
            pltpu.VMEM((seqs // 2, half, HD), F32),
            pltpu.VMEM((rows_of, half, HD), F32),
            pltpu.VMEM((2, half, HD), F32),
            pltpu.SemaphoreType.DMA((5,)),
            pltpu.SemaphoreType.DMA((2,)),
            pltpu.SemaphoreType.DMA((2,)),
            pltpu.SemaphoreType.DMA((2, chunks)),
            pltpu.SemaphoreType.DMA((2, chunks)),
            pltpu.SemaphoreType.DMA((2,)),
            pltpu.SemaphoreType.DMA((2,)),
            pltpu.SemaphoreType.DMA((2, chunks)),
            pltpu.SemaphoreType.DMA((2, chunks)),
            pltpu.SemaphoreType.DMA((2, chunks)),
            pltpu.SemaphoreType.DMA((2, chunks)),
            pltpu.SemaphoreType.DMA((2, chunks)),
            pltpu.SemaphoreType.DMA((2, chunks)),
            pltpu.SemaphoreType.DMA((max(teams - 1, 1),)),
            pltpu.SemaphoreType.DMA((max(teams - 1, 1),)),
            pltpu.SemaphoreType.DMA((max(seqs // 2 - 1, 1),)),
            pltpu.SemaphoreType.DMA((seqs // 2,)),
            pltpu.SemaphoreType.DMA((max(rows_of - 1, 1),)),
            pltpu.SemaphoreType.DMA((rows_of,)),
            pltpu.SemaphoreType.DMA((2,)),
            pltpu.SemaphoreType.REGULAR((8, 2)),
        ],
        compiler_params=pltpu.CompilerParams(
            collective_id=0, has_side_effects=True, vmem_limit_bytes=63 * 1024 * 1024
        ),
    )(
        queries,
        keys_in,
        values_in,
        grad_output,
        jnp.swapaxes(log_decay, 1, 2),
        lengths,
        norm_gain.reshape(heads, HD),
    )
    made = (query_grad, key_grad, value_grad, gain)
    any_space = pl.BlockSpec(memory_space=pltpu.VMEM)
    query_grad, key_grad, value_grad, gain = pl.pallas_call(
        deliver,
        out_shape=tuple(jax.ShapeDtypeStruct(one.shape, one.dtype) for one in made),
        in_specs=[any_space] * 4,
        out_specs=[any_space] * 4,
    )(*made)
    return query_grad, key_grad, value_grad, gain.reshape(features)


def solution(mesh):
    split = P("dp", "seq", "head")
    return jax.shard_map(
        functools.partial(on_device, mesh.shape["seq"], mesh.shape["head"], mesh.shape["dp"]),
        mesh=mesh,
        in_specs=(split, split, split, split, split, P("dp", None), P("head")),
        out_specs=(split, split, split, P("head")),
        check_vma=False,
    )
```

```python
import functools
import math

import jax
import jax.numpy as jnp
from jax import lax
from jax.experimental import pallas as pl
from jax.experimental.pallas import tpu as pltpu
from jax.sharding import PartitionSpec as P

EPSILON = 1e-06
HD = 128
TAG = 8
SPLIT = 2
UNROLL = 4
REACH = 4
MESH = pl.DeviceIdType.MESH
EXACT = lax.Precision.HIGHEST
F32 = jnp.float32
BF16 = jnp.bfloat16


def dot(left, right, over_left, over_right, precision=None):
    return lax.dot_general(
        left,
        right,
        (((over_left,), (over_right,)), ((), ())),
        preferred_element_type=F32,
        precision=precision,
    )


def each_head(body, start, count):
    def turn(step, carried):
        body([start + step * UNROLL + one for one in range(UNROLL)])
        return carried

    lax.fori_loop(0, count // UNROLL, turn, 0)


def kernel(
    seqs,
    teams,
    rows_of,
    q_hbm,
    k_hbm,
    v_hbm,
    up_hbm,
    log_hbm,
    lengths,
    gain_in,
    q_out,
    k_out,
    v_out,
    gain_out,
    q_ref,
    k_ref,
    v_ref,
    up_ref,
    log_ref,
    c_row,
    c_col,
    bias_ref,
    enter_ref,
    leave_ref,
    decay_ref,
    weight_ref,
    entered_ref,
    attn_ref,
    grad_ref,
    squares_ref,
    inner_ref,
    k_part,
    v_part,
    own_ref,
    peer_ref,
    step_in,
    carry_ref,
    chain_in,
    chain_out,
    pass_ref,
    far_ref,
    state_ref,
    sums_ref,
    sums_in,
    gain_row,
    gain_chips,
    gain_rows,
    gain_far,
    load_sem,
    pair_send,
    pair_recv,
    step_send,
    step_recv,
    carry_send,
    carry_recv,
    chain_send,
    chain_recv,
    back_send,
    back_recv,
    pass_send,
    pass_recv,
    sums_send,
    sums_recv,
    gain_chips_send,
    gain_chips_recv,
    gain_rows_send,
    gain_rows_recv,
    gain_far_sem,
    told_sem,
):
    blk, features = q_ref.shape
    heads = features // HD
    half = heads // 2
    chunks = half * SPLIT
    span = HD // SPLIT
    chips = seqs // 2
    seq = lax.axis_index("seq")
    team = lax.axis_index("head")
    place_z = lax.axis_index("dp")
    core = lax.rem(seq, 2)
    chip = lax.div(seq, 2)
    other = 1 - core
    peer = seq + 1 - 2 * core

    loads = [
        pltpu.make_async_copy(source.at[0], target, load_sem.at[slot])
        for slot, (source, target) in enumerate(
            [(log_hbm, log_ref), (k_hbm, k_ref), (v_hbm, v_ref), (q_hbm, q_ref), (up_hbm, up_ref)]
        )
    ]
    for load in loads:
        load.start()

    barrier = pltpu.get_barrier_semaphore()
    pl.semaphore_signal(barrier, inc=1, device_id={"seq": peer}, device_id_type=MESH)
    for step in range(1, teams):
        pl.semaphore_signal(
            barrier, inc=1, device_id={"head": lax.rem(team + step, teams)}, device_id_type=MESH
        )

    for step in range(1, chips):
        pl.semaphore_signal(
            barrier, inc=1, device_id={"seq": lax.rem(seq + 2 * step, seqs)}, device_id_type=MESH
        )

    def each_along_z(distance, action):
        for side, place in enumerate((place_z - distance, place_z + distance)):

            @pl.when(jnp.logical_and(place >= 0, place < rows_of))
            def _(side=side, place=place):
                action(side, place)

    close = min(REACH, rows_of - 1)
    for distance in range(1, close + 1):
        each_along_z(
            distance,
            lambda side, place: pl.semaphore_signal(
                barrier, inc=1, device_id={"dp": place}, device_id_type=MESH
            ),
        )
    greeted = 1 + teams - 1 + chips - 1
    for distance in range(1, close + 1):
        greeted = greeted + jnp.where(place_z >= distance, 1, 0)
        greeted = greeted + jnp.where(place_z + distance < rows_of, 1, 0)

    def tell(turn):
        each_along_z(
            REACH << turn,
            lambda side, place: pl.semaphore_signal(
                told_sem.at[turn, side], inc=1, device_id={"dp": place}, device_id_type=MESH
            ),
        )

    def hear(turn):
        each_along_z(
            REACH << turn, lambda side, place: pl.semaphore_wait(told_sem.at[turn, 1 - side], 1)
        )

    turns = 0
    while REACH << turns < rows_of:
        turns += 1

    def lanes(head):
        return pl.ds(pl.multiple_of(head * HD, HD), HD)

    row = lax.broadcasted_iota(jnp.int32, (blk, blk), 0)
    col = lax.broadcasted_iota(jnp.int32, (blk, blk), 1)
    triangle = (col <= row).astype(F32)
    places = []
    total = 0
    for one in range(lengths.shape[1] - 1):
        total = total + lengths[0, one]
        place = total - seq * blk
        places.append(jnp.where(place < 0, 2 * blk, place))
    at_row = lax.broadcasted_iota(jnp.int32, (blk, 1), 0)
    at_col = lax.broadcasted_iota(jnp.int32, (1, blk), 1)
    z_row = sum((at_row >= place).astype(jnp.int32) for place in places)
    z_col = sum((at_col >= place).astype(jnp.int32) for place in places)
    z_end = sum(jnp.where(place < blk, 1, 0) for place in places)
    loads[0].wait()
    log = log_ref[...]
    c_all = dot(triangle, log, 1, 1, EXACT)
    tail = c_all[blk - 1 : blk, :]
    leaving = jnp.exp(tail - c_all) * (z_row == z_end).astype(F32)
    carry = jnp.exp(tail) * jnp.where(z_end == 0, 1.0, 0.0)
    for head in range(heads):
        leave_ref[head] = jnp.broadcast_to(leaving[:, head : head + 1], (blk, HD))
        tag = jnp.broadcast_to(carry[:, head : head + 1], (TAG, HD))
        own_ref[0, head, HD : HD + TAG, :] = tag
        own_ref[1, head, HD : HD + TAG, :] = tag

    def block_state(group):
        made = []
        for head in group:
            left = (k_ref[:, lanes(head)].astype(F32) * leave_ref[head]).astype(BF16)
            made.append(dot(left, v_ref[:, lanes(head)], 0, 0))
        for head, value in zip(group, made):
            own_ref[0, head, 0:HD, :] = value

    def exchange(way):
        return pltpu.make_async_remote_copy(
            src_ref=own_ref.at[way, pl.ds(other * half, half)],
            dst_ref=peer_ref.at[way],
            send_sem=pair_send.at[way],
            recv_sem=pair_recv.at[way],
            device_id={"seq": peer},
            device_id_type=MESH,
        )

    def beside(way, chips_on):
        return lax.rem(seq + 2 * (chips_on if way == 0 else -chips_on) + seqs, seqs)

    def piece(way, index):
        start = pl.multiple_of(lax.rem(index, SPLIT) * span, span)
        return way, lax.div(index, SPLIT), pl.ds(start, span)

    def hand_on(way, index):
        return pltpu.make_async_remote_copy(
            src_ref=chain_out.at[piece(way, index)],
            dst_ref=step_in.at[piece(way, index)],
            send_sem=step_send.at[way, index],
            recv_sem=step_recv.at[way, index],
            device_id={"seq": beside(way, 1)},
            device_id_type=MESH,
        )

    def carried_on(way):
        return pltpu.make_async_remote_copy(
            src_ref=carry_ref.at[way, 0],
            dst_ref=carry_ref.at[way, 1],
            send_sem=carry_send.at[way],
            recv_sem=carry_recv.at[way],
            device_id={"seq": beside(way, 1)},
            device_id_type=MESH,
        )

    def ahead(way, index):
        return pltpu.make_async_remote_copy(
            src_ref=chain_out.at[piece(way, index)],
            dst_ref=chain_in.at[piece(way, index)],
            send_sem=chain_send.at[way, index],
            recv_sem=chain_recv.at[way, index],
            device_id={"seq": beside(way, 2)},
            device_id_type=MESH,
        )

    def back(way, index):
        return pltpu.make_async_remote_copy(
            src_ref=chain_in.at[piece(way, index)],
            dst_ref=chain_in.at[piece(way, index)],
            send_sem=back_send.at[way, index],
            recv_sem=back_recv.at[way, index],
            device_id={"seq": beside(way, -1)},
            device_id_type=MESH,
        )

    def across(way, index):
        return pltpu.make_async_remote_copy(
            src_ref=pass_ref.at[piece(way, index)],
            dst_ref=far_ref.at[piece(way, index)],
            send_sem=pass_send.at[way, index],
            recv_sem=pass_recv.at[way, index],
            device_id={"seq": peer},
            device_id_type=MESH,
        )

    def each_chunk(body):
        def turn(index, carried):
            body(index)
            return carried

        lax.fori_loop(0, chunks, turn, 0)

    ways = []
    for way in (0, 1):
        order = chip if way == 0 else chips - 1 - chip
        second = lax.rem(order, 2) == 1
        inner = order >= 2
        ways.append(
            (
                core == way,
                second,
                jnp.logical_not(second),
                inner,
                jnp.logical_and(second, inner),
                jnp.logical_and(jnp.logical_not(second), inner),
                jnp.logical_and(second, order < chips - 1),
                jnp.logical_and(second, order == 1),
            )
        )

    def join(way):
        lead, second, opening = ways[way][:3]
        exchange(way).wait_recv()

        def joined(local, carried):
            mine = own_ref[way, core * half + local, 0:HD, :]
            theirs = peer_ref[way, local, 0:HD, :]
            my_carry = own_ref[way, core * half + local, HD : HD + 1, :]
            their_carry = peer_ref[way, local, HD : HD + 1, :]
            carry_ref[way, 0, pl.ds(local, 1), :] = my_carry * their_carry
            chain_out[way, local] = jnp.where(
                lead, their_carry * mine + theirs, my_carry * theirs + mine
            )
            return carried

        lax.fori_loop(0, half, joined, 0)

        @pl.when(opening)
        def _():
            each_chunk(lambda index: hand_on(way, index).start())
            carried_on(way).start()
            step_in[way] = jnp.zeros(step_in.shape[1:], F32)
            carry_ref[way, 1] = jnp.ones(carry_ref.shape[2:], F32)

    def pair_up(way):
        second, onward, inner = ways[way][1], ways[way][6], ways[way][3]

        @pl.when(second)
        def _():
            carried_on(way).wait_recv()

            def body(index):
                at = piece(way, index)
                hand_on(way, index).wait_recv()
                chain_out[at] = carry_ref[way, 0, pl.ds(at[1], 1), :] * step_in[at] + chain_out[at]

                @pl.when(jnp.logical_and(onward, jnp.logical_not(inner)))
                def _():
                    ahead(way, index).start()

            each_chunk(body)

        @pl.when(jnp.logical_not(inner))
        def _():
            chain_in[way] = jnp.zeros(chain_in.shape[1:], F32)

    def chain(way):
        lead, second, opening, inner, second_inner, opening_inner, onward, seed = ways[way]

        def body(index):
            at = piece(way, index)
            local, rows = at[1:]

            @pl.when(second_inner)
            def _():
                ahead(way, index).wait_recv()

                @pl.when(onward)
                def _():
                    both = carry_ref[way, 0, pl.ds(local, 1), :] * carry_ref[way, 1, pl.ds(local, 1), :]
                    chain_out[at] = both * chain_in[at] + chain_out[at]
                    ahead(way, index).start()

                back(way, index).start()

            @pl.when(opening_inner)
            def _():
                back(way, index).wait_recv()

            my_carry = own_ref[way, core * half + local, HD : HD + 1, :]
            their_carry = peer_ref[way, local, HD : HD + 1, :]
            state = carry_ref[way, 1, pl.ds(local, 1), :] * chain_in[at] + step_in[at]
            mine = own_ref[way, core * half + local, rows, :]
            theirs = peer_ref[way, local, rows, :]
            middle = jnp.where(lead, my_carry * state + mine, their_carry * state + theirs)
            pass_ref[at] = jnp.where(lead, middle, state)
            across(way, index).start()
            state_ref[way, core * half + local, rows, :] = jnp.where(lead, state, middle).astype(BF16)

        each_chunk(body)

    def receive(way):
        def land(index):
            at = piece(way, index)
            across(way, index).wait_recv()
            state_ref[way, other * half + at[1], at[2], :] = far_ref[at].astype(BF16)

        each_chunk(land)

    loads[1].wait()
    loads[2].wait()
    each_head(block_state, other * half, half)
    pl.semaphore_wait(barrier, greeted)
    exchange(0).start()
    if turns:
        tell(0)
    each_head(block_state, core * half, half)

    c_row[...] = dot(log, triangle, 1, 1, EXACT)
    entering = jnp.exp(c_all) * (z_row == 0).astype(F32)
    for head in range(heads):
        enter_ref[head] = jnp.broadcast_to(entering[:, head : head + 1], (blk, HD))
        c_col[head] = jnp.broadcast_to(c_all[:, head : head + 1], (blk, HD))
    bias_ref[...] = jnp.where((z_row == z_col) & (col <= row), 0.0, -1e30)
    loads[3].wait()
    loads[4].wait()

    def near(group):
        made = []
        for head in group:
            query = q_ref[:, lanes(head)]
            scores = dot(query, k_ref[:, lanes(head)], 1, 1)
            start = jnp.broadcast_to(c_col[head][:, 0:1], (blk, blk))
            decay = jnp.exp(start - c_row[pl.ds(head, 1), :] + bias_ref[...])
            weight = (scores * decay).astype(BF16)
            entered = (query.astype(F32) * enter_ref[head]).astype(BF16)
            made.append((decay, weight, entered, dot(weight, v_ref[:, lanes(head)], 1, 0)))
        for head, (decay, weight, entered, value) in zip(group, made):
            decay_ref[head] = decay
            weight_ref[head] = weight
            entered_ref[head] = entered
            attn_ref[head] = value

    join(0)

    @pl.when(ways[0][3])
    def _():
        each_head(near, 0, heads)

    pair_up(0)
    chain(0)

    @pl.when(jnp.logical_not(ways[0][3]))
    def _():
        each_head(near, 0, heads)

    for turn in range(1, turns):
        hear(turn - 1)
        tell(turn)

    squares_ref[...] = jnp.zeros_like(squares_ref)
    inner_ref[...] = jnp.zeros_like(inner_ref)

    def attend(group):
        squares, inner = squares_ref[...], inner_ref[...]
        made = []
        for head in group:
            attn = attn_ref[head] + dot(entered_ref[head], state_ref[0, head], 1, 0)
            scaled = up_ref[:, lanes(head)].astype(F32) * gain_in[pl.ds(head, 1), :]
            squares = squares + attn * attn
            inner = inner + scaled * attn
            made.append(attn)
        for head, attn in zip(group, made):
            attn_ref[head] = attn
        squares_ref[...] = squares
        inner_ref[...] = inner

    each_head(attend, core * half, half)
    receive(0)
    each_head(attend, other * half, half)
    ones = jnp.ones((8, HD), F32)
    sums_ref[0:8, :] = dot(ones, squares_ref[...], 1, 1, EXACT)
    sums_ref[8:16, :] = dot(ones, inner_ref[...], 1, 1, EXACT)
    shares = [
        pltpu.make_async_remote_copy(
            src_ref=sums_ref,
            dst_ref=sums_in.at[step - 1],
            send_sem=sums_send.at[step - 1],
            recv_sem=sums_recv.at[step - 1],
            device_id={"head": lax.rem(team + step, teams)},
            device_id_type=MESH,
        )
        for step in range(1, teams)
    ]
    for share in shares:
        share.start()
    for share in shares:
        share.wait_recv()
    sums = sums_ref[...]
    for step in range(1, teams):
        sums = sums + sums_in[step - 1]
    width = features * teams
    chosen = lax.broadcasted_iota(jnp.int32, (8, HD), 0)
    chosen = jnp.where(chosen == 0, 1.0, 0.0).astype(F32)
    squares = dot(sums[0:8, :], chosen, 0, 0, EXACT)
    inner = dot(sums[8:16, :], chosen, 0, 0, EXACT)
    recip = lax.rsqrt(squares / width + EPSILON)
    squares_ref[...] = recip
    inner_ref[...] = recip * recip * recip * inner / width

    def gradient(group):
        recip, coef = squares_ref[...], inner_ref[...]
        made = []
        for head in group:
            attn = attn_ref[head]
            upstream = up_ref[:, lanes(head)].astype(F32)
            scaled = upstream * gain_in[pl.ds(head, 1), :]
            grad = (recip * scaled - coef * attn).astype(BF16)
            part = jnp.sum(upstream * attn * recip, axis=0, keepdims=True)
            made.append((grad, part, dot(entered_ref[head], grad, 0, 0)))
        for head, (grad, part, value) in zip(group, made):
            grad_ref[head] = grad
            gain_row[pl.ds(head, 1), :] = part
            own_ref[1, head, HD + 1 : HD + 2, :] = part
            own_ref[1, head, 0:HD, :] = value

    each_head(gradient, other * half, half)
    exchange(1).start()
    each_head(gradient, core * half, half)

    def masked(group):
        made = []
        for head in group:
            grad = grad_ref[head]
            raw = dot(grad, v_ref[:, lanes(head)], 1, 1)
            mask = (raw * decay_ref[head]).astype(BF16)
            query = dot(mask, k_ref[:, lanes(head)], 1, 0)
            query = query + enter_ref[head] * dot(grad, state_ref[0, head], 1, 1)
            made.append(
                (
                    query.astype(BF16),
                    dot(mask, q_ref[:, lanes(head)], 0, 0),
                    dot(weight_ref[head], grad, 0, 0),
                )
            )
        for head, (query, key, value) in zip(group, made):
            q_out[0, :, lanes(head)] = query
            k_part[head] = key
            v_part[head] = value

    def over_chips(step):
        to = lax.rem(chip + step, chips)
        return pltpu.make_async_remote_copy(
            src_ref=gain_chips.at[chip],
            dst_ref=gain_chips.at[chip],
            send_sem=gain_chips_send.at[step - 1],
            recv_sem=gain_chips_recv.at[chip],
            device_id={"seq": 2 * to + core},
            device_id_type=MESH,
        )

    def from_chips(step):
        place = lax.rem(chip + step, chips)
        return pltpu.make_async_remote_copy(
            src_ref=gain_chips.at[place],
            dst_ref=gain_chips.at[place],
            send_sem=gain_chips_send.at[step - 1],
            recv_sem=gain_chips_recv.at[place],
            device_id={"seq": 2 * place + core},
            device_id_type=MESH,
        )

    def over_rows(step):
        return pltpu.make_async_remote_copy(
            src_ref=gain_rows.at[place_z],
            dst_ref=gain_rows.at[place_z],
            send_sem=gain_rows_send.at[step - 1],
            recv_sem=gain_rows_recv.at[place_z],
            device_id={"dp": lax.rem(place_z + step, rows_of)},
            device_id_type=MESH,
        )

    def from_rows(step):
        place = lax.rem(place_z + step, rows_of)
        return pltpu.make_async_remote_copy(
            src_ref=gain_rows.at[place],
            dst_ref=gain_rows.at[place],
            send_sem=gain_rows_send.at[step - 1],
            recv_sem=gain_rows_recv.at[place],
            device_id={"dp": place},
            device_id_type=MESH,
        )

    def each_step(stop, action):
        def turn(step, carried):
            action(step)
            return carried

        lax.fori_loop(1, stop, turn, 0)

    def gain_begin():
        for local in range(half):
            gain_chips[chip, local : local + 1, :] = (
                gain_row[pl.ds(core * half + local, 1), :] + peer_ref[1, local, HD + 1 : HD + 2, :]
            )
        each_step(chips, lambda step: over_chips(step).start())

    def gain_middle():
        if turns:
            hear(turns - 1)
        each_step(chips, lambda step: from_chips(step).wait_recv())
        total = gain_chips[0]
        for one in range(1, chips):
            total = total + gain_chips[one]
        gain_rows[place_z] = total
        each_step(rows_of, lambda step: over_rows(step).start())

    gain_pass = pltpu.make_async_remote_copy(
        src_ref=gain_far.at[0],
        dst_ref=gain_far.at[1],
        send_sem=gain_far_sem.at[0],
        recv_sem=gain_far_sem.at[1],
        device_id={"seq": peer},
        device_id_type=MESH,
    )

    def gain_end():
        each_step(rows_of, lambda step: from_rows(step).wait_recv())
        total = gain_rows[0]
        for one in range(1, rows_of):
            total = total + gain_rows[one]
        gain_far[0] = total / math.sqrt(blk * seqs * rows_of)
        gain_pass.start()

    far_on = ways[1][3]

    @pl.when(far_on)
    def _():
        each_head(masked, 0, half)

    join(1)
    gain_begin()

    @pl.when(far_on)
    def _():
        each_head(masked, half, half)

    pair_up(1)

    @pl.when(far_on)
    def _():
        gain_middle()

    chain(1)

    @pl.when(jnp.logical_not(far_on))
    def _():
        gain_middle()
        each_head(masked, 0, heads)

    last = chips - 1 - chip >= 4

    @pl.when(last)
    def _():
        gain_end()

    def finish(group):
        made = []
        for head in group:
            state = state_ref[1, head]
            leave = leave_ref[head]
            key = k_part[head] + leave * dot(v_ref[:, lanes(head)], state, 1, 1)
            value = v_part[head] + leave * dot(k_ref[:, lanes(head)], state, 1, 0)
            made.append((key.astype(BF16), value.astype(BF16)))
        for head, (key, value) in zip(group, made):
            k_out[0, :, lanes(head)] = key
            v_out[0, :, lanes(head)] = value

    each_head(finish, core * half, half)
    receive(1)
    each_head(finish, other * half, half)

    @pl.when(jnp.logical_not(last))
    def _():
        gain_end()


    gain_pass.wait_recv()
    for local in range(half):
        gain_out[pl.ds(core * half + local, 1), :] = gain_far[0, local : local + 1, :]
        gain_out[pl.ds(other * half + local, 1), :] = gain_far[1, local : local + 1, :]
    gain_pass.wait_send()
    each_step(chips, lambda step: over_chips(step).wait_send())
    each_step(rows_of, lambda step: over_rows(step).wait_send())
    for share in shares:
        share.wait_send()
    for way in (0, 1):
        exchange(way).wait_send()
        opening, second_inner, onward = ways[way][2], ways[way][4], ways[way][6]

        @pl.when(opening)
        def _(way=way):
            carried_on(way).wait_send()
            each_chunk(lambda index: hand_on(way, index).wait_send())

        @pl.when(onward)
        def _(way=way):
            each_chunk(lambda index: ahead(way, index).wait_send())

        @pl.when(second_inner)
        def _(way=way):
            each_chunk(lambda index: back(way, index).wait_send())

        each_chunk(lambda index, way=way: across(way, index).wait_send())


def deliver(*refs):
    count = len(refs) // 2
    for one in range(count):
        refs[count + one][...] = refs[one][...]


def on_device(seqs, teams, rows_of, queries, keys_in, values_in, grad_output, log_decay, lengths, norm_gain):
    tokens, features = queries.shape[1:]
    heads = log_decay.shape[2]
    half = heads // 2
    chunks = half * SPLIT
    whole = jax.ShapeDtypeStruct((1, tokens, features), BF16)
    anywhere = pl.BlockSpec(memory_space=pltpu.HBM)
    vmem = pl.BlockSpec(memory_space=pltpu.VMEM)
    wide = pltpu.VMEM((heads, tokens, HD), F32)
    states = pltpu.VMEM((2, half, HD, HD), F32)
    query_grad, key_grad, value_grad, gain = pl.pallas_call(
        functools.partial(kernel, seqs, teams, rows_of),
        out_shape=(whole, whole, whole, jax.ShapeDtypeStruct((heads, HD), F32)),
        in_specs=[anywhere] * 5 + [pl.BlockSpec(memory_space=pltpu.SMEM), vmem],
        out_specs=[vmem] * 4,
        scratch_shapes=[
            pltpu.VMEM((tokens, features), BF16),
            pltpu.VMEM((tokens, features), BF16),
            pltpu.VMEM((tokens, features), BF16),
            pltpu.VMEM((tokens, features), BF16),
            pltpu.VMEM((heads, tokens), F32),
            pltpu.VMEM((heads, tokens), F32),
            wide,
            pltpu.VMEM((tokens, tokens), F32),
            wide,
            wide,
            pltpu.VMEM((heads, tokens, tokens), F32),
            pltpu.VMEM((heads, tokens, tokens), BF16),
            pltpu.VMEM((heads, tokens, HD), BF16),
            wide,
            pltpu.VMEM((heads, tokens, HD), BF16),
            pltpu.VMEM((tokens, HD), F32),
            pltpu.VMEM((tokens, HD), F32),
            wide,
            wide,
            pltpu.VMEM((2, heads, HD + TAG, HD), F32),
            pltpu.VMEM((2, half, HD + TAG, HD), F32),
            states,
            pltpu.VMEM((2, 2, half, HD), F32),
            states,
            states,
            states,
            states,
            pltpu.VMEM((2, heads, HD, HD), BF16),
            pltpu.VMEM((16, tokens), F32),
            pltpu.VMEM((max(teams - 1, 1), 16, tokens), F32),
            pltpu.VMEM((heads, HD), F32),
            pltpu.VMEM((seqs // 2, half, HD), F32),
            pltpu.VMEM((rows_of, half, HD), F32),
            pltpu.VMEM((2, half, HD), F32),
            pltpu.SemaphoreType.DMA((5,)),
            pltpu.SemaphoreType.DMA((2,)),
            pltpu.SemaphoreType.DMA((2,)),
            pltpu.SemaphoreType.DMA((2, chunks)),
            pltpu.SemaphoreType.DMA((2, chunks)),
            pltpu.SemaphoreType.DMA((2,)),
            pltpu.SemaphoreType.DMA((2,)),
            pltpu.SemaphoreType.DMA((2, chunks)),
            pltpu.SemaphoreType.DMA((2, chunks)),
            pltpu.SemaphoreType.DMA((2, chunks)),
            pltpu.SemaphoreType.DMA((2, chunks)),
            pltpu.SemaphoreType.DMA((2, chunks)),
            pltpu.SemaphoreType.DMA((2, chunks)),
            pltpu.SemaphoreType.DMA((max(teams - 1, 1),)),
            pltpu.SemaphoreType.DMA((max(teams - 1, 1),)),
            pltpu.SemaphoreType.DMA((max(seqs // 2 - 1, 1),)),
            pltpu.SemaphoreType.DMA((seqs // 2,)),
            pltpu.SemaphoreType.DMA((max(rows_of - 1, 1),)),
            pltpu.SemaphoreType.DMA((rows_of,)),
            pltpu.SemaphoreType.DMA((2,)),
            pltpu.SemaphoreType.REGULAR((8, 2)),
        ],
        compiler_params=pltpu.CompilerParams(
            collective_id=0, has_side_effects=True, vmem_limit_bytes=63 * 1024 * 1024
        ),
    )(
        queries,
        keys_in,
        values_in,
        grad_output,
        jnp.swapaxes(log_decay, 1, 2),
        lengths,
        norm_gain.reshape(heads, HD),
    )
    made = (query_grad, key_grad, value_grad, gain)
    any_space = pl.BlockSpec(memory_space=pltpu.VMEM)
    query_grad, key_grad, value_grad, gain = pl.pallas_call(
        deliver,
        out_shape=tuple(jax.ShapeDtypeStruct(one.shape, one.dtype) for one in made),
        in_specs=[any_space] * 4,
        out_specs=[any_space] * 4,
    )(*made)
    return query_grad, key_grad, value_grad, gain.reshape(features)


def solution(mesh):
    split = P("dp", "seq", "head")
    return jax.shard_map(
        functools.partial(on_device, mesh.shape["seq"], mesh.shape["head"], mesh.shape["dp"]),
        mesh=mesh,
        in_specs=(split, split, split, split, split, P("dp", None), P("head")),
        out_specs=(split, split, split, P("head")),
        check_vma=False,
    )
```
